32 devices in a mesh: region: 4 (over y, x), sub: 8 (over z, core).
Axes of the slice: x: 2, y: 2, z: 4, core: 2. Of those that a mesh axis runs over, the one named last changes fastest.
Arguments:
- scalars: float32 [4096, 128], P(('region', 'sub')), may hold values from -6 to 6
- vectors: float32 [3, 4096, 128], P(None, ('region', 'sub')), may hold values from -6 to 6
- positions: float32 [3, 4096], P(None, ('region', 'sub')), may hold values from 0 to 8
- pair_blocks: int32 [2, 48], replicated, may hold values from 0 to 31, as said below
- pair_mask: int32 [48, 547], replicated, may hold values from 0 to 1073741823
- wavevectors: float32 [3, 512], replicated, may hold values from -2 to 2
- message_in: float32 [2, 128, 128], replicated, may hold values from -0.5 to 0.5
- message_out: float32 [2, 128, 384], replicated, may hold values from -0.5 to 0.5
- filter_weight: float32 [2, 20, 384], replicated, may hold values from -0.3125 to 0.3125
- ewald_weight: float32 [2, 128, 128], replicated, may hold values from -0.5 to 0.5
- ewald_filter: float32 [2, 512, 128], replicated, may hold values from -6 to 6
- mixing_left: float32 [2, 128, 128], replicated, may hold values from -0.5 to 0.5
- mixing_right: float32 [2, 128, 128], replicated, may hold values from -0.5 to 0.5
- update_in: float32 [2, 256, 128], replicated, may hold values from -0.375 to 0.375
- update_out: float32 [2, 128, 384], replicated, may hold values from -0.5 to 0.5
Outputs:
- scalars_out: float32 [4096, 128], P(('region', 'sub'))
- vectors_out: float32 [3, 4096, 128], P(None, ('region', 'sub'))
The draws below stay inside these ranges and needn't reach their ends.
Inputs may be any that keep to these rules, and one draw needn't show every extreme that they name: `pair_blocks`: pairs are listed region by region, 12 pairs for each of the 4 regions of 8 consecutive blocks. Both blocks of a pair lie in the same region, the first below the second; no pair is listed twice, and within a region the first blocks never fall along the list.
All inputs are finite; a program needn't handle non-finite values.
Results may differ from the reference program's by a relative error of at most 0.0003.
Values sent between devices are 32-bit elements; how exact they have to be, the bound alone decides.
No kernel may reach another device: no remote copies, remote signals or barrier semaphores. Data moves between devices by JAX's collectives and lax.ppermute only.
A program may use at most 128 MiB of HBM per device.

```python
import math
import jax
import jax.numpy as jnp
import numpy as np
from jax import lax

F = 128
NRBF = 20
BS = 128
KW = 512
LAYERS = 2
REGIONS = 4
REGION_BLOCKS = 8
NATOM = 4096
RPAIRS = 12
PAIRS = 48
MASKW = 547


def pair_table(key):
    upper_first, upper_second = np.triu_indices(REGION_BLOCKS, 1)
    first_table = jnp.asarray(upper_first.astype(np.int32))
    second_table = jnp.asarray(upper_second.astype(np.int32))
    combos = upper_first.shape[0]
    corner = REGION_BLOCKS - 2
    firsts = []
    seconds = []
    for region in range(REGIONS):
        others = jax.random.permutation(jax.random.fold_in(key, 11 + region), combos - 1)[:RPAIRS - 1]
        others = others + (others >= corner).astype(others.dtype)
        chosen = jnp.concatenate([others, jnp.full((1,), corner, others.dtype)])
        chosen = jnp.sort(chosen)
        firsts.append(first_table[chosen] + region * REGION_BLOCKS)
        seconds.append(second_table[chosen] + region * REGION_BLOCKS)
    return jnp.stack([jnp.concatenate(firsts), jnp.concatenate(seconds)]).astype(jnp.int32)


def draw_pair_blocks(key, part):
    return pair_table(key)


def place_ends(values, rng, smallest, top_value):
    extent = values.shape
    index_at = [jax.random.randint(jax.random.fold_in(rng, axis), (), 0, extent[axis]) for axis in range(len(extent))]
    values = values.at[tuple(index_at)].set(smallest)
    longest = extent.index(max(extent))
    index_at[longest] = (index_at[longest] + 1) % extent[longest]
    return values.at[tuple(index_at)].set(top_value)


def steps_of(stream_key, shape, shards, low, largest):
    def one(axis_at, shards_of):
        heights = jax.random.uniform(jax.random.fold_in(jax.random.fold_in(stream_key, 6), axis_at), (shards_of,), jnp.float32, low / len(shards), largest / len(shards))
        return jnp.repeat(jnp.exp(heights), shape[axis_at] // shards_of).reshape((-1,) + (1,) * (len(shape) - axis_at - 1))

    gain = one(*shards[0])
    for cut in shards[1:]:
        gain = gain * one(*cut)
    return gain


def gaussian(stream_key, shape, width, limit, shards=(), kind=jnp.bfloat16):
    result = jax.random.normal(stream_key, shape, jnp.float32) * width
    if len(shards) > 0:
        result = steps_of(stream_key, shape, shards, -0.22, 0.18) * result
    return jnp.clip(result, min=-limit, max=limit).astype(kind)


def setup_inputs(seed: int = 0) -> dict:
    streams_of = jax.random.split(jax.random.key(seed), 16)
    scalars = gaussian(streams_of[0], (NATOM, F), 1.0, 6.0, ((0, 32),), jnp.float32)
    vectors = gaussian(streams_of[1], (3, NATOM, F), 1.0, 6.0, ((1, 32),), jnp.float32)
    positions = jnp.clip(8.0 * jax.random.uniform(streams_of[2], (3, NATOM), jnp.float32) ** steps_of(streams_of[2], (3, NATOM), ((1, 32),), -0.2, 0.2), 0.0, 8.0)
    pair_blocks = draw_pair_blocks(jax.random.fold_in(streams_of[15], 71), 0)
    pair_mask = place_ends(jax.random.randint(streams_of[4], (PAIRS, MASKW), 0, 1073741824), jax.random.fold_in(streams_of[4], 1), 0, 1073741823).astype(jnp.int32)
    wavevectors = jnp.clip(jax.random.uniform(streams_of[5], (3, KW), jnp.float32, -2.0, 2.0), -2.0, 2.0)
    message_in = gaussian(streams_of[6], (LAYERS, F, F), F ** -0.5, 0.5, (), jnp.float32)
    message_out = gaussian(streams_of[7], (LAYERS, F, 3 * F), F ** -0.5, 0.5, (), jnp.float32)
    filter_weight = gaussian(streams_of[8], (LAYERS, NRBF, 3 * F), (16 * NRBF) ** -0.5, 0.3125, (), jnp.float32)
    ewald_weight = gaussian(streams_of[9], (LAYERS, F, F), F ** -0.5, 0.5, (), jnp.float32)
    ewald_filter = gaussian(streams_of[10], (LAYERS, KW, F), 1.0, 6.0, (), jnp.float32)
    mixing_left = gaussian(streams_of[11], (LAYERS, F, F), F ** -0.5, 0.5, (), jnp.float32)
    mixing_right = gaussian(streams_of[12], (LAYERS, F, F), F ** -0.5, 0.5, (), jnp.float32)
    update_in = gaussian(streams_of[13], (LAYERS, 2 * F, F), (2 * F) ** -0.5, 0.375, (), jnp.float32)
    update_out = gaussian(streams_of[14], (LAYERS, F, 3 * F), F ** -0.5, 0.5, (), jnp.float32)
    return {"scalars": scalars, "vectors": vectors, "positions": positions, "pair_blocks": pair_blocks, "pair_mask": pair_mask, "wavevectors": wavevectors, "message_in": message_in, "message_out": message_out, "filter_weight": filter_weight, "ewald_weight": ewald_weight, "ewald_filter": ewald_filter, "mixing_left": mixing_left, "mixing_right": mixing_right, "update_in": update_in, "update_out": update_out}


HIGHEST = lax.Precision.HIGHEST
CUTOFF = 8.0

def unpack_mask(packed):
    shifts = jnp.arange(30, dtype=jnp.int32)
    unpacked = jnp.right_shift(packed[:, None], shifts[None, :]) & 1
    return unpacked.reshape(-1)[:BS * BS].reshape(BS, BS).astype(jnp.float32)

def geometry(pos_first, pos_second, packed):
    offset = pos_second[:, None, :] - pos_first[:, :, None]
    distance = jnp.sqrt(lax.optimization_barrier(jnp.sum(offset * offset, axis=0)) + 1.0)
    direction = offset / distance[None]
    spacing = CUTOFF / (NRBF - 1)
    centers = jnp.arange(NRBF, dtype=jnp.float32) * spacing
    scaled = (distance[None] - centers[:, None, None]) / spacing
    radial = jnp.exp(-0.5 * scaled * scaled) * unpack_mask(packed)[None]
    return (radial, direction)

def side_terms(radial, direction, source, filters):
    channels = source.shape[1] // 5
    rows = radial.shape[1]
    product = jnp.dot(radial.reshape(-1, radial.shape[2]), source, precision=HIGHEST)
    product = product.reshape(NRBF, rows, 5 * channels)
    steered = (direction[:, None] * radial[None]).reshape(-1, radial.shape[2])
    turned = jnp.dot(steered, source[:, 4 * channels:], precision=HIGHEST).reshape(3, NRBF, rows, channels)
    w_scalar = filters[:, :channels]
    w_vector = filters[:, channels:2 * channels]
    w_radial = filters[:, 2 * channels:]
    delta_scalar = jnp.einsum('kic,kc->ic', product[..., :channels], w_scalar, precision=HIGHEST)
    parts = []
    for component in range(3):
        lower = (1 + component) * channels
        along = jnp.einsum('kic,kc->ic', product[..., lower:lower + channels], w_vector, precision=HIGHEST)
        along = along + jnp.einsum('kic,kc->ic', turned[component], w_radial, precision=HIGHEST)
        parts.append(along)
    return (delta_scalar, jnp.stack(parts))

def pair_terms(radial, direction, source_first, source_second, filters):
    to_first = side_terms(radial, direction, source_second, filters)
    to_second = side_terms(radial.transpose(0, 2, 1), -direction.transpose(0, 2, 1), source_first, filters)
    return (to_first, to_second)

def message_sources(scalars_now, vectors_now, first_weight, second_weight):
    channels = scalars_now.shape[1]
    hidden = jax.nn.silu(jnp.dot(scalars_now, first_weight, precision=HIGHEST))
    filt_in = jnp.dot(hidden, second_weight, precision=HIGHEST)
    phi_vector = filt_in[:, channels:2 * channels]
    return jnp.concatenate([filt_in[:, :channels], phi_vector * vectors_now[0], phi_vector * vectors_now[1], phi_vector * vectors_now[2], filt_in[:, 2 * channels:]], axis=1)

def update_block(mid_scalars, mid_vectors, left_weight, right_weight, gate_in, gate_out):
    channels = mid_scalars.shape[1]
    flat = mid_vectors.reshape(-1, channels)
    left = jnp.dot(flat, left_weight, precision=HIGHEST).reshape(mid_vectors.shape)
    right = jnp.dot(flat, right_weight, precision=HIGHEST).reshape(mid_vectors.shape)
    vec_norm = jnp.sqrt(lax.optimization_barrier(jnp.sum(right * right, axis=0)) + 1.0)
    hidden = jax.nn.silu(jnp.dot(jnp.concatenate([mid_scalars, vec_norm], axis=1), gate_in, precision=HIGHEST))
    gates = jnp.dot(hidden, gate_out, precision=HIGHEST)
    new_vectors = mid_vectors + gates[None, :, :channels] * left
    new_scalars = mid_scalars + gates[:, channels:2 * channels] * lax.optimization_barrier(jnp.sum(left * right, axis=0)) + gates[:, 2 * channels:]
    return (new_scalars, new_vectors)

def add_rows(target, delta, row_at, axis_id):
    current = lax.dynamic_slice_in_dim(target, row_at, BS, axis_id)
    return lax.dynamic_update_slice_in_dim(target, current + delta, row_at, axis_id)

def reference(scalars, vectors, positions, pair_blocks, pair_mask, wavevectors, message_in, message_out, filter_weight, ewald_weight, ewald_filter, mixing_left, mixing_right, update_in, update_out):
    natoms = scalars.shape[0]
    phases = jnp.dot(wavevectors.T, positions, precision=HIGHEST)
    cosines = jnp.cos(phases)
    sines = jnp.sin(phases)
    scale = 1.0 / math.sqrt(natoms * KW)
    scalars_now, vectors_now = (scalars, vectors)
    for layer_id in range(LAYERS):
        sources = message_sources(scalars_now, vectors_now, message_in[layer_id], message_out[layer_id])
        filters = filter_weight[layer_id]

        def visit(pair_id, totals):
            sum_scalar, sum_vector = totals
            first_row = (pair_blocks[0, pair_id] * BS).astype(jnp.int32)
            second_row = (pair_blocks[1, pair_id] * BS).astype(jnp.int32)
            pos_first = lax.dynamic_slice_in_dim(positions, first_row, BS, 1)
            pos_second = lax.dynamic_slice_in_dim(positions, second_row, BS, 1)
            radial, direction = geometry(pos_first, pos_second, pair_mask[pair_id])
            source_first = lax.dynamic_slice_in_dim(sources, first_row, BS, 0)
            source_second = lax.dynamic_slice_in_dim(sources, second_row, BS, 0)
            to_first, to_second = pair_terms(radial, direction, source_first, source_second, filters)
            sum_scalar = add_rows(sum_scalar, to_first[0], first_row, 0)
            sum_scalar = add_rows(sum_scalar, to_second[0], second_row, 0)
            sum_vector = add_rows(sum_vector, to_first[1], first_row, 1)
            sum_vector = add_rows(sum_vector, to_second[1], second_row, 1)
            return (sum_scalar, sum_vector)
        start = (jnp.zeros(scalars_now.shape, jnp.float32), jnp.zeros(vectors_now.shape, jnp.float32))
        delta_scalar, delta_vector = lax.fori_loop(0, pair_blocks.shape[1], visit, start)
        charges = jnp.dot(scalars_now, ewald_weight[layer_id], precision=HIGHEST)
        structure_re = jnp.dot(cosines, charges, precision=HIGHEST)
        structure_im = jnp.dot(sines, charges, precision=HIGHEST)
        ewald = jnp.dot(cosines.T, ewald_filter[layer_id] * structure_re, precision=HIGHEST)
        ewald = (ewald + jnp.dot(sines.T, ewald_filter[layer_id] * structure_im, precision=HIGHEST)) * scale
        mid_scalars = scalars_now + delta_scalar + ewald
        mid_vectors = vectors_now + delta_vector
        scalars_now, vectors_now = update_block(mid_scalars, mid_vectors, mixing_left[layer_id], mixing_right[layer_id], update_in[layer_id], update_out[layer_id])
    return (scalars_now, vectors_now)
```

```python
import functools
import math

import jax
import jax.numpy as jnp
import numpy as np
from jax import lax
from jax.experimental import pallas as pl
from jax.experimental.pallas import tpu as pltpu
from jax.sharding import PartitionSpec as P

NRBF = 20
BS = 128
KW = 512
LAYERS = 2
BITS = 30
CUTOFF = 8.0
SPACING = CUTOFF / (NRBF - 1)
CENTER = 0.5 * CUTOFF
VMEM = 58 * 1024 * 1024
F32 = jnp.float32
BF16 = jnp.bfloat16


def split(x):
    high = x.astype(BF16)
    return high, (x - high.astype(F32)).astype(BF16)


def wide_left(x):
    high, low = split(x)
    return jnp.concatenate([high, low, high], axis=1)


def wide_right(x):
    high, low = split(x)
    return jnp.concatenate([high, high, low], axis=0)


def stacked(x):
    high, low = split(x)
    return jnp.concatenate([high, high], axis=0), low


def dot(a, b):
    return jnp.dot(a, b, preferred_element_type=F32)


def dot3(a, b):
    return dot(wide_left(a), wide_right(b))


def silu(x):
    return x / (1.0 + jnp.exp(-x))


def turn_fits():
    nodes = 0.5 * np.cos(np.pi * (np.arange(400) + 0.5) / 400)
    cheb = np.polynomial.chebyshev
    fit_cos = cheb.Chebyshev.fit(nodes * nodes, np.cos(2 * np.pi * nodes), 7, domain=[0, 0.25])
    fit_sin = cheb.Chebyshev.fit(nodes * nodes, np.sinc(2 * nodes) * 2 * np.pi, 7, domain=[0, 0.25])
    to_poly = lambda fit: [float(c) for c in fit.convert(kind=np.polynomial.Polynomial).coef]
    return to_poly(fit_cos), to_poly(fit_sin)


COS_FIT, SIN_FIT = turn_fits()


def horner(coefs, x):
    total = jnp.full_like(x, coefs[-1])
    for c in coefs[-2::-1]:
        total = total * x + c
    return total


def cos_sin(turns):
    rest = turns - jnp.round(turns)
    square = rest * rest
    return horner(COS_FIT, square), horner(SIN_FIT, square) * rest


def columns_of(pos):
    return jnp.transpose(pos)


def cost(flops, moved, exps=0):
    return pl.CostEstimate(flops=int(flops), bytes_accessed=int(moved), transcendentals=int(exps))


def fixed(shape, *at):
    at = tuple(at) + (0,) * (len(shape) - len(at))
    return pl.BlockSpec(shape, lambda *_: at)


SMEM_SPEC = pl.BlockSpec(memory_space=pltpu.SMEM)


def meta_kernel(n_sub, per_region, slots, ids_ref, pairs_ref, meta_ref):
    region, sub = ids_ref[0], ids_ref[1]
    base = region * per_region
    for row in range(5):
        for slot in range(slots):
            meta_ref[row, slot] = 0

    def visit(p, found):
        first = pairs_ref[0, base + p] - region * n_sub
        second = pairs_ref[1, base + p] - region * n_sub
        hit = (first == sub) | (second == sub)

        @pl.when(hit & (found < slots))
        def _():
            other = jnp.where(first == sub, second, first)
            meta_ref[1, found] = base + p
            meta_ref[2, found] = other ^ sub
            meta_ref[3, found] = (first == sub).astype(jnp.int32)
            meta_ref[4, found] = other

        return found + hit.astype(jnp.int32)

    meta_ref[0, 0] = lax.fori_loop(0, per_region, visit, jnp.int32(0))


def find_pairs(ids, pair_blocks, n_sub, per_region, slots):
    return pl.pallas_call(
        functools.partial(meta_kernel, n_sub, per_region, slots),
        in_specs=[SMEM_SPEC, SMEM_SPEC],
        out_specs=SMEM_SPEC,
        out_shape=jax.ShapeDtypeStruct((5, slots), jnp.int32),
    )(ids, pair_blocks)


def at_pair(step, meta_ref):
    return (jnp.maximum(jnp.minimum(step, (meta_ref[0, 0] - 1) // 2), 0), 0, 0)


def near_dots(tables, rows, sources):
    number = len(sources)
    values = [tables[i, rows, :] for i in range(number)]
    highs = [v[:, :BS] for v in values]
    both = [b for b, _ in sources]
    low = [l for _, l in sources]
    return dot(jnp.concatenate(values, axis=1), jnp.concatenate(both, axis=0)) + dot(
        jnp.concatenate(highs, axis=1), jnp.concatenate(low, axis=0)
    )


def add_terms(totals, cols, tables, sources, weight):
    group = 4
    total = totals[:, cols]
    for k in range(0, NRBF, group):
        product = near_dots(tables, slice(k * BS, (k + group) * BS), sources)
        for g in range(group):
            total = total + product[g * BS : (g + 1) * BS] * weight[k + g : k + g + 1]
    totals[:, cols] = total


def one_or_two(step, count, act):
    for number in (1, 2):
        here = (2 * step + 1 == count) if number == 1 else (2 * step + 1 < count)
        pl.when(here)(functools.partial(act, number))


def radial_tables(meta_ref, listed, at, near, pos_ref, masks_ref, radial_ref, over_ref):
    pair = meta_ref[1, listed]
    slot = meta_ref[2, listed]
    is_first = meta_ref[3, listed]
    words = masks_ref[pl.ds(pair, 1), :]
    tiles = -(-words.shape[1] // BS)
    rest = tiles * BS - words.shape[1]
    if rest:
        words = jnp.concatenate([words, jnp.zeros((1, rest), jnp.int32)], axis=1)
    row = lax.broadcasted_iota(jnp.int32, (BS, BS), 0)
    row_tile = (row * 2185) >> 16
    spread = jnp.zeros((BS, BS), jnp.int32)
    for tile in range(tiles):
        spread = jnp.where(
            row_tile == tile,
            jnp.broadcast_to(words[:, tile * BS : (tile + 1) * BS], (BS, BS)),
            spread,
        )
    spot = (row - row_tile * BITS) * BS + lax.broadcasted_iota(jnp.int32, (BS, BS), 1)
    index = (spot * 34953) >> 20
    picked = jnp.take_along_axis(spread, index, axis=1)
    mask = (jnp.right_shift(picked, spot - index * BITS) & 1).astype(F32)
    mask = jnp.where(is_first == 1, mask, jnp.transpose(mask))
    source = jnp.zeros((8, BS), F32)
    for e in range(1, len(near)):
        source = jnp.where(slot == e, near[e][...], source)
    mine = columns_of(pos_ref[...])
    square = jnp.zeros((BS, BS), F32)
    for d in range(3):
        offset = source[d : d + 1, :] - mine[:, d : d + 1]
        square = square + offset * offset
    distance = jnp.sqrt(square + 1.0)
    inverse = 1.0 / distance
    root = math.sqrt(0.5 * math.log2(math.e))
    scaled = jnp.where(mask > 0.5, distance * (root / SPACING), 1.0e4)
    for k in range(NRBF):
        gap = scaled - k * root
        radial = jnp.exp2(-(gap * gap))
        rows = slice(k * BS, (k + 1) * BS)
        for ref, value in ((radial_ref, radial), (over_ref, radial * inverse)):
            high, low = split(value)
            ref[at, rows, 0:BS] = high
            ref[at, rows, BS : 2 * BS] = low


def early_kernel(n_sub, build, meta_ref, *refs):
    blocks, refs = refs[:n_sub], refs[n_sub:]
    places, refs = refs[:n_sub], refs[n_sub:]
    if build:
        in_ref, out_ref, filter_ref, masks_ref, partial_ref, phi_ref, radial_ref, over_ref, sources, totals = refs
    else:
        in_ref, out_ref, filter_ref, over_ref, partial_ref, phi_ref, sources, totals = refs
    step = pl.program_id(0)
    count = meta_ref[0, 0]

    @pl.when(step == 0)
    def _():
        totals[...] = jnp.zeros_like(totals)
        scalars = jnp.concatenate([blocks[e][...] for e in range(1, n_sub)], axis=0)
        hidden = silu(dot3(scalars, in_ref[0]))
        phi = dot3(hidden, out_ref[0])
        for e in range(1, n_sub):
            rows = phi[(e - 1) * BS : e * BS]
            phi_ref[e - 1] = rows[:, : 2 * BS]
            phi_r = rows[:, 2 * BS :]
            place = columns_of(places[e][...])
            parts = [phi_r] + [phi_r * (place[:, d : d + 1] - CENTER) for d in range(3)]
            for at, part in enumerate(parts):
                high, low = split(part)
                cols = slice(at * BS, (at + 1) * BS)
                sources[e - 1, 0:BS, cols] = high
                sources[e - 1, BS : 2 * BS, cols] = high
                sources[e - 1, 2 * BS :, cols] = low

    def act(number):
        if build:
            for i in range(number):
                radial_tables(meta_ref, 2 * step + i, i, places, places[0], masks_ref, radial_ref, over_ref)
        weight = filter_ref[0, :, 2 * BS :]
        weight = jnp.concatenate([weight, weight], axis=1)
        slot = [meta_ref[2, 2 * step + i] - 1 for i in range(number)]
        for tile in range(2):
            cols = slice(tile * 2 * BS, (tile + 1) * 2 * BS)
            near = [(sources[e, : 2 * BS, cols], sources[e, 2 * BS :, cols]) for e in slot]
            add_terms(totals, cols, over_ref, near, weight)

    one_or_two(step, count, act)

    @pl.when(step == pl.num_programs(0) - 1)
    def _():
        mine = columns_of(places[0][...])
        for d in range(3):
            partial_ref[d * BS : (d + 1) * BS, :] = (
                totals[:, (1 + d) * BS : (2 + d) * BS] - (mine[:, d : d + 1] - CENTER) * totals[:, :BS]
            )


def early_terms(meta, layer, blocks, spots, weights, masks=None, over=None):
    n_sub = len(blocks)
    slots = meta.shape[1]
    build = over is None
    table = pl.BlockSpec((2, NRBF * BS, 2 * BS), at_pair)
    shape = jax.ShapeDtypeStruct((slots, NRBF * BS, 2 * BS), BF16)
    out_specs = [fixed((3 * BS, BS)), fixed((n_sub - 1, BS, 2 * BS))]
    out_shape = [
        jax.ShapeDtypeStruct((3 * BS, BS), F32),
        jax.ShapeDtypeStruct((n_sub - 1, BS, 2 * BS), F32),
    ]
    return pl.pallas_call(
        functools.partial(early_kernel, n_sub, build),
        grid_spec=pltpu.PrefetchScalarGridSpec(
            num_scalar_prefetch=1,
            grid=(meta.shape[1] // 2,),
            in_specs=[fixed((BS, BS))] * n_sub
            + [fixed((8, BS), BS // 8)] * n_sub
            + [fixed((1,) + w.shape[1:], layer) for w in weights]
            + ([fixed(masks.shape)] if build else [table]),
            out_specs=out_specs + ([table, table] if build else []),
            scratch_shapes=[
                pltpu.VMEM((n_sub - 1, 3 * BS, 4 * BS), BF16),
                pltpu.VMEM((BS, 4 * BS), F32),
            ],
        ),
        out_shape=out_shape + ([shape, shape] if build else []),
        compiler_params=pltpu.CompilerParams(vmem_limit_bytes=VMEM),
        cost_estimate=cost(3 * 4 * NRBF * BS * BS * 4 * BS * 2 * 3, 10e6),
    )(meta, *blocks, *spots, *weights, masks if build else over)


def own_trig_kernel(waves_ref, place_ref, own_ref):
    waves = waves_ref[...] * (1.0 / (2.0 * math.pi))
    mine = columns_of(place_ref[...])
    turns = jnp.zeros((BS, waves.shape[1]), F32)
    for d in range(3):
        turns = turns + mine[:, d : d + 1] * waves[d : d + 1, :]
    own_ref[...] = jnp.concatenate(split(jnp.concatenate(cos_sin(turns), axis=1)), axis=1)


def own_trig_of(waves, spot):
    return pl.pallas_call(
        own_trig_kernel,
        grid=(1,),
        in_specs=[fixed(waves.shape), fixed((8, BS), BS // 8)],
        out_specs=fixed((BS, 4 * KW)),
        out_shape=jax.ShapeDtypeStruct((BS, 4 * KW), BF16),
        compiler_params=pltpu.CompilerParams(vmem_limit_bytes=VMEM),
        cost_estimate=cost(BS * KW * 40, 1e6),
    )(waves, spot)


def structure_kernel(n_sub, build, *refs):
    if build:
        ids_ref, waves_ref, refs = refs[0], refs[1], refs[2:]
        places, refs = refs[:n_sub], refs[n_sub:]
    blocks, refs = refs[:n_sub], refs[n_sub:]
    atoms = n_sub * BS
    if build:
        weight_ref, out_ref, trig_ref = refs
        waves = waves_ref[...] * (1.0 / (2.0 * math.pi))
        rows = waves.shape[1] // 2
        waves = jnp.where(ids_ref[1] % 2 == 0, waves[:, :rows], waves[:, rows:])
        half = jnp.transpose(jnp.concatenate([waves, jnp.zeros((5, rows), F32)], axis=0))
        for e in range(n_sub):
            place = places[e][...]
            turns = jnp.zeros((rows, BS), F32)
            for d in range(3):
                turns = turns + half[:, d : d + 1] * place[d : d + 1, :]
            for at, value in enumerate(cos_sin(turns)):
                block = slice(at * rows, (at + 1) * rows)
                for part, piece in enumerate(split(value)):
                    trig_ref[block, part * atoms + e * BS : part * atoms + (e + 1) * BS] = piece
    else:
        weight_ref, trig_ref, out_ref = refs
    both, low = stacked(jnp.concatenate([blocks[e][...] for e in range(n_sub)], axis=0))
    total = dot(trig_ref[...], both) + dot(trig_ref[:, :atoms], low)
    out_ref[...] = dot3(total, weight_ref[0])


def structure(layer, blocks, weight, ids=None, waves=None, spots=None, region_trig=None):
    n_sub = len(blocks)
    build = region_trig is None
    trig_shape = (KW, 2 * n_sub * BS)
    charges = [fixed((BS, BS))] * n_sub + [fixed((1,) + weight.shape[1:], layer)]
    out_shape = [jax.ShapeDtypeStruct((KW, BS), F32)]
    if build:
        in_specs = [SMEM_SPEC, fixed(waves.shape)] + [fixed((8, BS), BS // 8)] * n_sub + charges
        operands = (ids, waves, *spots, *blocks, weight)
        out_shape += [jax.ShapeDtypeStruct(trig_shape, BF16)]
    else:
        in_specs = charges + [fixed(trig_shape)]
        operands = (*blocks, weight, region_trig)
    return pl.pallas_call(
        functools.partial(structure_kernel, n_sub, build),
        grid=(1,),
        in_specs=in_specs,
        out_specs=[fixed(s.shape) for s in out_shape],
        out_shape=out_shape,
        compiler_params=pltpu.CompilerParams(vmem_limit_bytes=VMEM),
        cost_estimate=cost(KW * n_sub * BS * BS * 6, 4e6),
    )(*operands)


def late_kernel(
    scale, n_sub, meta_ref, ids_ref, scalars_ref, vectors_ref, phi_a_ref, phi_b_ref, radial_ref, partial_ref, *refs
):
    blocks, refs = refs[: n_sub - 1], refs[n_sub - 1 :]
    (
    mine_ref, other_ref, own_ref, factor_ref, filter_ref, left_ref, right_ref, gate_in_ref, gate_out_ref,
    new_scalars_ref, new_vectors_ref, totals,
    ) = refs
    step = pl.program_id(0)
    count = meta_ref[0, 0]

    @pl.when(step == 0)
    def _():
        totals[:, :BS] = jnp.zeros((BS, BS), F32)
        for d in range(3):
            totals[:, (1 + d) * BS : (2 + d) * BS] = partial_ref[d * BS : (d + 1) * BS, :]

    def act(number):
        w_s, w_v = filter_ref[0, :, :BS], filter_ref[0, :, BS : 2 * BS]
        parts = []
        for i, phi_ref in enumerate((phi_a_ref, phi_b_ref)[:number]):
            slot = meta_ref[2, 2 * step + i]
            near = blocks[0][...]
            for e in range(2, n_sub):
                near = jnp.where(slot == e, blocks[e - 1][...], near)
            phi_s, phi_v = phi_ref[0, :, :BS], phi_ref[0, :, BS:]
            parts.append([phi_s] + [phi_v * near[d * BS : (d + 1) * BS, :] for d in range(3)])
        for tile, names in enumerate(((w_s, w_v), (w_v, w_v))):
            cols = slice(tile * 2 * BS, (tile + 1) * 2 * BS)
            sources = [stacked(jnp.concatenate(p[2 * tile : 2 * tile + 2], axis=1)) for p in parts]
            add_terms(totals, cols, radial_ref, sources, jnp.concatenate(names, axis=1))

    one_or_two(step, count, act)

    @pl.when(step == pl.num_programs(0) - 1)
    def _():
        lower = ids_ref[1] % 2 == 0
        mine, other = mine_ref[...], other_ref[...]
        half = mine.shape[0] // 2
        first = jnp.where(lower, mine, other)
        second = jnp.where(lower, other, mine)
        factors = factor_ref[0] * scale
        both, low = stacked(
            jnp.concatenate(
                [
                    first[:half] * factors[:half],
                    second[:half] * factors[half:],
                    first[half:] * factors[:half],
                    second[half:] * factors[half:],
                ],
                axis=0,
            )
        )
        ewald = dot(own_ref[...], both) + dot(own_ref[:, : 2 * KW], low)
        mid_scalars = scalars_ref[...] + totals[:, :BS] + ewald
        mid_vectors = jnp.concatenate(
            [vectors_ref[d] + totals[:, (1 + d) * BS : (2 + d) * BS] for d in range(3)], axis=0
        )
        mixed = dot3(mid_vectors, jnp.concatenate([left_ref[0], right_ref[0]], axis=1))
        left, right = mixed[:, :BS], mixed[:, BS:]
        parts = [slice(d * BS, (d + 1) * BS) for d in range(3)]
        norm = jnp.sqrt(sum(right[p] * right[p] for p in parts) + 1.0)
        along = sum(left[p] * right[p] for p in parts)
        hidden = silu(dot3(jnp.concatenate([mid_scalars, norm], axis=1), gate_in_ref[0]))
        gates = dot3(hidden, gate_out_ref[0])
        g_v, g_sv, g_s = (gates[:, i * BS : (i + 1) * BS] for i in range(3))
        new_scalars_ref[...] = mid_scalars + g_sv * along + g_s
        for d, p in enumerate(parts):
            new_vectors_ref[d] = mid_vectors[p] + g_v * left[p]


def late_terms(meta, ids, layer, scale, scalars, vectors, phi, near, radial, partial, mine, other, own, weights):
    n_sub = len(near)

    def at_other(i, step, meta_ref):
        listed = jnp.minimum(2 * at_pair(step, meta_ref)[0] + i, meta_ref[0, 0] - 1)
        return (jnp.maximum(meta_ref[2, jnp.maximum(listed, 0)] - 1, 0), 0, 0)

    return pl.pallas_call(
        functools.partial(late_kernel, scale, n_sub),
        grid_spec=pltpu.PrefetchScalarGridSpec(
            num_scalar_prefetch=1,
            grid=(meta.shape[1] // 2,),
            in_specs=[
                SMEM_SPEC,
                fixed(scalars.shape),
                fixed(vectors.shape),
                pl.BlockSpec((1, BS, 2 * BS), functools.partial(at_other, 0)),
                pl.BlockSpec((1, BS, 2 * BS), functools.partial(at_other, 1)),
                pl.BlockSpec((2, NRBF * BS, 2 * BS), at_pair),
                fixed(partial.shape),
            ]
            + [fixed(b.shape) for b in near[1:]]
            + [
                fixed(mine.shape),
                fixed(other.shape),
                fixed(own.shape),
            ]
            + [fixed((1,) + w.shape[1:], layer) for w in weights],
            out_specs=[fixed(scalars.shape), fixed(vectors.shape)],
            scratch_shapes=[pltpu.VMEM((BS, 4 * BS), F32)],
        ),
        out_shape=[
            jax.ShapeDtypeStruct(scalars.shape, F32),
            jax.ShapeDtypeStruct(vectors.shape, F32),
        ],
        compiler_params=pltpu.CompilerParams(vmem_limit_bytes=VMEM),
        cost_estimate=cost(3 * 4 * NRBF * BS * BS * 4 * BS * 2 * 3, 10e6),
    )(meta, ids, scalars, vectors, phi, phi, radial, partial, *near[1:], mine, other, own, *weights)


def exchange(x, axis, mask):
    size = lax.axis_size(axis)
    return lax.ppermute(x, axis, [(i, i ^ mask) for i in range(size)])


def gather(x):
    n_sub = lax.axis_size("sub")
    parts = [None] * n_sub
    for e in range(0, n_sub, 2):
        parts[e] = x if e == 0 else exchange(x, "sub", e)
    for e in range(0, n_sub, 2):
        parts[e + 1] = exchange(parts[e], "sub", 1)
    return parts


def after(x, *others):
    return lax.optimization_barrier((x, *others))[0]


def body(
    scalars,
    vectors,
    positions,
    pair_blocks,
    pair_mask,
    wavevectors,
    message_in,
    message_out,
    filter_weight,
    ewald_weight,
    ewald_filter,
    mixing_left,
    mixing_right,
    update_in,
    update_out,
):
    n_region = lax.axis_size("region")
    n_sub = lax.axis_size("sub")
    natoms = BS * n_region * n_sub
    scale = 1.0 / math.sqrt(natoms * KW)
    per_region = pair_blocks.shape[1] // n_region
    slots = -(-min(n_sub - 1, per_region) // 2) * 2
    ids = jnp.stack([lax.axis_index("region"), lax.axis_index("sub")]).astype(jnp.int32)
    place = jnp.pad(positions, ((0, 8 - positions.shape[0]), (0, 0)))
    send = jnp.concatenate([scalars, place], axis=0)
    meta = find_pairs(ids, pair_blocks, n_sub, per_region, slots)
    own_trig = own_trig_of(wavevectors, send)
    radial = over = region_trig = spots = None
    for layer in range(LAYERS):
        blocks = gather(send)
        near = gather(vectors.reshape(3 * BS, -1))
        if layer == 0:
            spots = blocks
            first_ids = after(ids, meta, own_trig)
            partial, region_trig = structure(layer, blocks, ewald_weight, first_ids, wavevectors, spots)
        else:
            (partial,) = structure(layer, blocks, ewald_weight, region_trig=region_trig)
        others = [exchange(partial, "region", mask) for mask in range(1, n_region)]
        weights = (message_in, message_out, filter_weight)
        turn = after(meta, partial)
        if layer == 0:
            along, phi, radial, over = early_terms(turn, layer, blocks, spots, weights, masks=pair_mask)
        else:
            along, phi = early_terms(turn, layer, blocks, spots, weights, over=over)
        *others, along = lax.optimization_barrier((*others, along))
        mine = sum(others, partial)
        theirs = exchange(mine, "sub", 1)
        scalars, vectors = late_terms(
            meta, ids, layer, scale, scalars, vectors, phi, near, radial, along, mine, theirs, own_trig,
            (ewald_filter, filter_weight, mixing_left, mixing_right, update_in, update_out),
        )
        send = scalars
    return scalars, vectors


def solution(mesh):
    placed = (
        P(("region", "sub"), None),
        P(None, ("region", "sub"), None),
        P(None, ("region", "sub")),
    ) + (P(),) * 12
    return jax.shard_map(
        body,
        mesh=mesh,
        in_specs=placed,
        out_specs=(P(("region", "sub"), None), P(None, ("region", "sub"), None)),
        check_vma=False,
    )
```

```python
import functools
import math

import jax
import jax.numpy as jnp
import numpy as np
from jax import lax
from jax.experimental import pallas as pl
from jax.experimental.pallas import tpu as pltpu
from jax.sharding import PartitionSpec as P

NRBF = 20
BS = 128
KW = 512
LAYERS = 2
BITS = 30
CUTOFF = 8.0
SPACING = CUTOFF / (NRBF - 1)
CENTER = 0.5 * CUTOFF
VMEM = 44 * 1024 * 1024
WINDOW = 1e10
F32 = jnp.float32
BF16 = jnp.bfloat16


def split(x):
    high = x.astype(BF16)
    return high, (x - high.astype(F32)).astype(BF16)


def wide_left(x):
    high, low = split(x)
    return jnp.concatenate([high, low, high], axis=1)


def wide_right(x):
    high, low = split(x)
    return jnp.concatenate([high, high, low], axis=0)


def stacked(x):
    high, low = split(x)
    return jnp.concatenate([high, high], axis=0), low


def dot(a, b):
    return jnp.dot(a, b, preferred_element_type=F32)


def dot3(a, b):
    return dot(wide_left(a), wide_right(b))


def silu(x):
    return x / (1.0 + jnp.exp(-x))


def turn_fits():
    nodes = 0.5 * np.cos(np.pi * (np.arange(400) + 0.5) / 400)
    cheb = np.polynomial.chebyshev
    fit_cos = cheb.Chebyshev.fit(nodes * nodes, np.cos(2 * np.pi * nodes), 7, domain=[0, 0.25])
    fit_sin = cheb.Chebyshev.fit(nodes * nodes, np.sinc(2 * nodes) * 2 * np.pi, 7, domain=[0, 0.25])
    to_poly = lambda fit: [float(c) for c in fit.convert(kind=np.polynomial.Polynomial).coef]
    return to_poly(fit_cos), to_poly(fit_sin)


COS_FIT, SIN_FIT = turn_fits()


def horner(coefs, x):
    total = jnp.full_like(x, coefs[-1])
    for c in coefs[-2::-1]:
        total = total * x + c
    return total


def cos_sin(turns):
    rest = turns - jnp.round(turns)
    square = rest * rest
    return horner(COS_FIT, square), horner(SIN_FIT, square) * rest


def columns_of(pos):
    return jnp.transpose(pos)


def cost(flops, moved, exps=0):
    return pl.CostEstimate(flops=int(flops), bytes_accessed=int(moved), transcendentals=int(exps))


SMEM_SPEC = pl.BlockSpec(memory_space=pltpu.SMEM)
VMEM_SPEC = pl.BlockSpec(memory_space=pltpu.VMEM)
HBM_SPEC = pl.BlockSpec(memory_space=pltpu.HBM)


def meta_kernel(n_sub, per_region, slots, ids_ref, pairs_ref, meta_ref):
    region, sub = ids_ref[0], ids_ref[1]
    base = region * per_region
    for row in range(5):
        for slot in range(slots):
            meta_ref[row, slot] = lax.rem(sub, 2) if row == 4 else 0

    def visit(p, found):
        first = pairs_ref[0, base + p] - region * n_sub
        second = pairs_ref[1, base + p] - region * n_sub
        hit = (first == sub) | (second == sub)

        @pl.when(hit & (found < slots))
        def _():
            other = jnp.where(first == sub, second, first)
            meta_ref[1, found] = base + p
            meta_ref[2, found] = other ^ sub
            meta_ref[3, found] = (first == sub).astype(jnp.int32)

        return found + hit.astype(jnp.int32)

    meta_ref[0, 0] = lax.fori_loop(0, per_region, visit, jnp.int32(0))


def find_pairs(ids, pair_blocks, n_sub, per_region, slots):
    return pl.pallas_call(
        functools.partial(meta_kernel, n_sub, per_region, slots),
        in_specs=[SMEM_SPEC, SMEM_SPEC],
        out_specs=SMEM_SPEC,
        out_shape=jax.ShapeDtypeStruct((5, slots), jnp.int32),
    )(ids, pair_blocks)


def near_dots(tables, rows, sources):
    number = len(sources)
    values = [tables[i, rows, :] for i in range(number)]
    highs = [v[:, :BS] for v in values]
    both = [b for b, _ in sources]
    low = [l for _, l in sources]
    return dot(jnp.concatenate(values, axis=1), jnp.concatenate(both, axis=0)) + dot(
        jnp.concatenate(highs, axis=1), jnp.concatenate(low, axis=0)
    )


def add_terms(totals, cols, tables, sources, weight):
    group = 4
    total = totals[:, cols]
    for k in range(0, NRBF, group):
        product = near_dots(tables, slice(k * BS, (k + group) * BS), sources)
        for g in range(group):
            total = total + product[g * BS : (g + 1) * BS] * weight[k + g : k + g + 1]
    totals[:, cols] = total


def one_or_two(step, count, act):
    for number in (1, 2):
        here = (2 * step + 1 == count) if number == 1 else (2 * step + 1 < count)
        pl.when(here)(functools.partial(act, number))


def table_copy(table, step, buffer, sems):
    slot = lax.rem(step, 2)
    return pltpu.make_async_copy(table.at[pl.ds(2 * step, 2)], buffer.at[slot], sems.at[slot])


def over_tables(count, table, buffer, sems, act):
    steps = (count + 1) // 2

    def one(step, carry):
        @pl.when(step + 1 < steps)
        def _():
            table_copy(table, step + 1, buffer, sems).start()

        table_copy(table, step, buffer, sems).wait()
        act(step, buffer.at[lax.rem(step, 2)])
        return carry

    lax.fori_loop(0, steps, one, 0)


def fill_tables(count, tables, act):
    steps = (count + 1) // 2

    def out(step, table, buffer, sems):
        slot = lax.rem(step, 2)
        return pltpu.make_async_copy(buffer.at[slot], table.at[pl.ds(2 * step, 2)], sems.at[slot])

    def one(step, carry):
        @pl.when(step >= 2)
        def _():
            for t in tables:
                out(step - 2, *t).wait()

        act(step, [buffer.at[lax.rem(step, 2)] for _, buffer, _ in tables])
        for t in tables:
            out(step, *t).start()
        return carry

    lax.fori_loop(0, steps, one, 0)
    for back in (2, 1):

        @pl.when(steps >= back)
        def _():
            for t in tables:
                out(steps - back, *t).wait()


def radial_tables(meta_ref, listed, at, near, pos_ref, masks_ref, radial_ref, over_ref):
    pair = meta_ref[1, listed]
    slot = meta_ref[2, listed]
    is_first = meta_ref[3, listed]
    words = masks_ref[pl.ds(pair, 1), :]
    tiles = -(-words.shape[1] // BS)
    rest = tiles * BS - words.shape[1]
    if rest:
        words = jnp.concatenate([words, jnp.zeros((1, rest), jnp.int32)], axis=1)
    row = lax.broadcasted_iota(jnp.int32, (BS, BS), 0)
    row_tile = (row * 2185) >> 16
    spread = jnp.zeros((BS, BS), jnp.int32)
    for tile in range(tiles):
        spread = jnp.where(
            row_tile == tile,
            jnp.broadcast_to(words[:, tile * BS : (tile + 1) * BS], (BS, BS)),
            spread,
        )
    spot = (row - row_tile * BITS) * BS + lax.broadcasted_iota(jnp.int32, (BS, BS), 1)
    index = (spot * 34953) >> 20
    picked = jnp.take_along_axis(spread, index, axis=1)
    mask = (jnp.right_shift(picked, spot - index * BITS) & 1).astype(F32)
    mask = jnp.where(is_first == 1, mask, jnp.transpose(mask))
    source = jnp.zeros((8, BS), F32)
    for e in range(1, len(near)):
        source = jnp.where(slot == e, near[e][...], source)
    mine = columns_of(pos_ref[...])
    square = jnp.zeros((BS, BS), F32)
    for d in range(3):
        offset = source[d : d + 1, :] - mine[:, d : d + 1]
        square = square + offset * offset
    distance = jnp.sqrt(square + 1.0)
    inverse = 1.0 / distance
    root = math.sqrt(0.5 * math.log2(math.e))
    scaled = jnp.where(mask > 0.5, distance * (root / SPACING), 1.0e4)
    for k in range(NRBF):
        gap = scaled - k * root
        radial = jnp.exp2(-(gap * gap))
        rows = slice(k * BS, (k + 1) * BS)
        for ref, value in ((radial_ref, radial), (over_ref, radial * inverse)):
            high, low = split(value)
            ref[at, rows, 0:BS] = high
            ref[at, rows, BS : 2 * BS] = low


def early_kernel(n_sub, build, layer, meta_ref, *refs):
    blocks, refs = [r.at[:BS, :] for r in refs[:n_sub]], refs[n_sub:]
    places, refs = [r.at[r.shape[0] - 8 :, :] for r in refs[:n_sub]], refs[n_sub:]
    if build:
        in_ref, out_ref, filter_ref, masks_ref, partial_ref, phi_ref, tables_hbm = refs[:7]
        sources, totals, over_buffer, over_sems, radial_buffer, radial_sems = refs[7:]
    else:
        in_ref, out_ref, filter_ref, tables_hbm, partial_ref, phi_ref, sources, totals, over_buffer, over_sems = refs
    radial_hbm, over_hbm = tables_hbm.at[0], tables_hbm.at[1]
    count = meta_ref[0, 0]
    if not build:

        @pl.when(count > 0)
        def _():
            table_copy(over_hbm, 0, over_buffer, over_sems).start()

    totals[...] = jnp.zeros_like(totals)
    scalars = jnp.concatenate([blocks[e][...] for e in range(1, n_sub)], axis=0)
    hidden = silu(dot3(scalars, in_ref[layer]))
    phi = dot3(hidden, out_ref[layer])
    for e in range(1, n_sub):
        rows = phi[(e - 1) * BS : e * BS]
        phi_ref[e - 1] = rows[:, : 2 * BS]
        phi_r = rows[:, 2 * BS :]
        place = columns_of(places[e][...])
        parts = [phi_r] + [phi_r * (place[:, d : d + 1] - CENTER) for d in range(3)]
        for at, part in enumerate(parts):
            high, low = split(part)
            cols = slice(at * BS, (at + 1) * BS)
            sources[e - 1, 0:BS, cols] = high
            sources[e - 1, BS : 2 * BS, cols] = high
            sources[e - 1, 2 * BS :, cols] = low

    weight = filter_ref[layer, :, 2 * BS :]
    weight = jnp.concatenate([weight, weight], axis=1)

    def terms(step, table, number):
        slot = [meta_ref[2, 2 * step + i] - 1 for i in range(number)]
        for tile in range(2):
            cols = slice(tile * 2 * BS, (tile + 1) * 2 * BS)
            near = [(sources[e, : 2 * BS, cols], sources[e, 2 * BS :, cols]) for e in slot]
            add_terms(totals, cols, table, near, weight)

    if build:

        def act(step, tables):
            radial, over = tables

            def both(number):
                for i in range(number):
                    radial_tables(meta_ref, 2 * step + i, i, places, places[0], masks_ref, radial, over)
                terms(step, over, number)

            one_or_two(step, count, both)

        fill_tables(
            count, ((radial_hbm, radial_buffer, radial_sems), (over_hbm, over_buffer, over_sems)), act
        )
    else:

        def act(step, table):
            one_or_two(step, count, functools.partial(terms, step, table))

        over_tables(count, over_hbm, over_buffer, over_sems, act)

    mine = columns_of(places[0][...])
    for d in range(3):
        partial_ref[d * BS : (d + 1) * BS, :] = (
            totals[:, (1 + d) * BS : (2 + d) * BS] - (mine[:, d : d + 1] - CENTER) * totals[:, :BS]
        )


def table_buffers(number):
    return [pltpu.VMEM((2, 2, NRBF * BS, 2 * BS), BF16), pltpu.SemaphoreType.DMA((2,))] * number


def early_terms(meta, layer, blocks, spots, weights, masks=None, tables=None):
    n_sub = len(blocks)
    slots = meta.shape[1]
    build = tables is None
    shape = jax.ShapeDtypeStruct((2, slots, NRBF * BS, 2 * BS), BF16)
    out_shape = [
        jax.ShapeDtypeStruct((3 * BS, BS), F32),
        jax.ShapeDtypeStruct((n_sub - 1, BS, 2 * BS), F32),
    ]
    return pl.pallas_call(
        functools.partial(early_kernel, n_sub, build, layer),
        in_specs=[SMEM_SPEC] + [VMEM_SPEC] * (2 * n_sub + 3) + [VMEM_SPEC if build else HBM_SPEC],
        out_specs=[VMEM_SPEC] * 2 + ([HBM_SPEC] if build else []),
        scratch_shapes=[
            pltpu.VMEM((n_sub - 1, 3 * BS, 4 * BS), BF16),
            pltpu.VMEM((BS, 4 * BS), F32),
        ]
        + table_buffers(2 if build else 1),
        out_shape=out_shape + ([shape] if build else []),
        compiler_params=pltpu.CompilerParams(vmem_limit_bytes=VMEM),
        cost_estimate=cost(3 * 4 * NRBF * BS * BS * 4 * BS * 2 * 3, 10e6),
    )(meta, *blocks, *spots, *weights, masks if build else tables)


def own_trig_kernel(waves_ref, place_ref, own_ref):
    waves = waves_ref[...] * (1.0 / (2.0 * math.pi))
    mine = columns_of(place_ref[BS:, :])
    turns = jnp.zeros((BS, waves.shape[1]), F32)
    for d in range(3):
        turns = turns + mine[:, d : d + 1] * waves[d : d + 1, :]
    own_ref[...] = jnp.concatenate(split(jnp.concatenate(cos_sin(turns), axis=1)), axis=1)


def own_trig_of(waves, spot):
    return pl.pallas_call(
        own_trig_kernel,
        in_specs=[VMEM_SPEC] * 2,
        out_specs=VMEM_SPEC,
        out_shape=jax.ShapeDtypeStruct((BS, 4 * KW), BF16),
        compiler_params=pltpu.CompilerParams(vmem_limit_bytes=VMEM),
        cost_estimate=cost(WINDOW, 1e6),
    )(waves, spot)


def structure_kernel(n_sub, build, layer, *refs):
    if build:
        meta_ref, waves_ref, refs = refs[0], refs[1], refs[2:]
        places = [r.at[r.shape[0] - 8 :, :] for r in refs[:n_sub]]
    blocks, refs = [r.at[:BS, :] for r in refs[:n_sub]], refs[n_sub:]
    atoms = n_sub * BS
    if build:
        weight_ref, out_ref, trig_ref = refs
        waves = waves_ref[...] * (1.0 / (2.0 * math.pi))
        rows = waves.shape[1] // 2
        waves = jnp.where(meta_ref[4, 0] == 0, waves[:, :rows], waves[:, rows:])
        half = jnp.transpose(jnp.concatenate([waves, jnp.zeros((5, rows), F32)], axis=0))
        for e in range(n_sub):
            place = places[e][...]
            turns = jnp.zeros((rows, BS), F32)
            for d in range(3):
                turns = turns + half[:, d : d + 1] * place[d : d + 1, :]
            for at, value in enumerate(cos_sin(turns)):
                block = slice(at * rows, (at + 1) * rows)
                for part, piece in enumerate(split(value)):
                    trig_ref[block, part * atoms + e * BS : part * atoms + (e + 1) * BS] = piece
    else:
        weight_ref, trig_ref, out_ref = refs
    both, low = stacked(jnp.concatenate([blocks[e][...] for e in range(n_sub)], axis=0))
    total = dot(trig_ref[...], both) + dot(trig_ref[:, :atoms], low)
    out_ref[...] = dot3(total, weight_ref[layer])


def structure(layer, blocks, weight, meta=None, waves=None, region_trig=None):
    n_sub = len(blocks)
    build = region_trig is None
    out_shape = [jax.ShapeDtypeStruct((KW, BS), F32)]
    if build:
        in_specs = [SMEM_SPEC] + [VMEM_SPEC] * (n_sub + 2)
        operands = (meta, waves, *blocks, weight)
        out_shape += [jax.ShapeDtypeStruct((KW, 2 * n_sub * BS), BF16)]
    else:
        in_specs = [VMEM_SPEC] * (n_sub + 2)
        operands = (*blocks, weight, region_trig)
    return pl.pallas_call(
        functools.partial(structure_kernel, n_sub, build, layer),
        in_specs=in_specs,
        out_specs=[VMEM_SPEC] * len(out_shape),
        out_shape=out_shape,
        compiler_params=pltpu.CompilerParams(vmem_limit_bytes=VMEM),
        cost_estimate=cost(KW * n_sub * BS * BS * 6, 4e6),
    )(*operands)


def late_kernel(scale, n_sub, layer, last, meta_ref, *refs):
    scalars_ref, vectors_ref, phi_ref, partial_ref, mine_ref, other_ref, own_ref = refs[:7]
    factor_ref, filter_ref, left_ref, right_ref, gate_in_ref, gate_out_ref = refs[7:13]
    near, refs = refs[13 : 12 + n_sub], refs[12 + n_sub :]
    radial_hbm, refs = refs[0].at[0], refs[1:]
    outs, (totals, buffer, sems) = refs[:-3], refs[-3:]
    count = meta_ref[0, 0]

    @pl.when(count > 0)
    def _():
        table_copy(radial_hbm, 0, buffer, sems).start()

    totals[:, :BS] = jnp.zeros((BS, BS), F32)
    for d in range(3):
        totals[:, (1 + d) * BS : (2 + d) * BS] = partial_ref[d * BS : (d + 1) * BS, :]
    w_s, w_v = filter_ref[layer, :, :BS], filter_ref[layer, :, BS : 2 * BS]

    def terms(step, table, number):
        parts = []
        for i in range(number):
            slot = meta_ref[2, 2 * step + i]
            vectors = near[0][...]
            for e in range(2, n_sub):
                vectors = jnp.where(slot == e, near[e - 1][...], vectors)
            phi = phi_ref[slot - 1]
            phi_s, phi_v = phi[:, :BS], phi[:, BS:]
            parts.append([phi_s] + [phi_v * vectors[d * BS : (d + 1) * BS, :] for d in range(3)])
        for tile, names in enumerate(((w_s, w_v), (w_v, w_v))):
            cols = slice(tile * 2 * BS, (tile + 1) * 2 * BS)
            sources = [stacked(jnp.concatenate(p[2 * tile : 2 * tile + 2], axis=1)) for p in parts]
            add_terms(totals, cols, table, sources, jnp.concatenate(names, axis=1))

    def act(step, table):
        one_or_two(step, count, functools.partial(terms, step, table))

    over_tables(count, radial_hbm, buffer, sems, act)

    lower = meta_ref[4, 0] == 0
    mine, other = mine_ref[...], other_ref[...]
    half = mine.shape[0] // 2
    first = jnp.where(lower, mine, other)
    second = jnp.where(lower, other, mine)
    factors = factor_ref[layer] * scale
    both, low = stacked(
        jnp.concatenate(
            [
                first[:half] * factors[:half],
                second[:half] * factors[half:],
                first[half:] * factors[:half],
                second[half:] * factors[half:],
            ],
            axis=0,
        )
    )
    ewald = dot(own_ref[...], both) + dot(own_ref[:, : 2 * KW], low)
    mid_scalars = scalars_ref[...] + totals[:, :BS] + ewald
    mid_vectors = jnp.concatenate(
        [vectors_ref[d * BS : (d + 1) * BS, :] + totals[:, (1 + d) * BS : (2 + d) * BS] for d in range(3)], axis=0
    )
    mixed = dot3(mid_vectors, jnp.concatenate([left_ref[layer], right_ref[layer]], axis=1))
    left, right = mixed[:, :BS], mixed[:, BS:]
    parts = [slice(d * BS, (d + 1) * BS) for d in range(3)]
    norm = jnp.sqrt(sum(right[p] * right[p] for p in parts) + 1.0)
    along = sum(left[p] * right[p] for p in parts)
    hidden = silu(dot3(jnp.concatenate([mid_scalars, norm], axis=1), gate_in_ref[layer]))
    gates = dot3(hidden, gate_out_ref[layer])
    g_v, g_sv, g_s = (gates[:, i * BS : (i + 1) * BS] for i in range(3))
    new_scalars = mid_scalars + g_sv * along + g_s
    new_vectors = [mid_vectors[p] + g_v * left[p] for p in parts]
    if last:
        outs[0][...] = new_scalars
        for d in range(3):
            outs[1][d] = new_vectors[d]
    else:
        outs[0][...] = new_scalars
        for d, p in enumerate(parts):
            outs[1][p, :] = new_vectors[d]


def late_terms(meta, layer, last, scale, scalars, vectors, phi, near, tables, partial, mine, other, own, weights):
    n_sub = len(near)
    shapes = [(BS, BS), (3, BS, BS)] if last else [(BS, BS), (3 * BS, BS)]
    return pl.pallas_call(
        functools.partial(late_kernel, scale, n_sub, layer, last),
        in_specs=[SMEM_SPEC] + [VMEM_SPEC] * (12 + n_sub) + [HBM_SPEC],
        out_specs=[VMEM_SPEC] * len(shapes),
        scratch_shapes=[pltpu.VMEM((BS, 4 * BS), F32)] + table_buffers(1),
        out_shape=[jax.ShapeDtypeStruct(shape, F32) for shape in shapes],
        compiler_params=pltpu.CompilerParams(vmem_limit_bytes=VMEM),
        cost_estimate=cost(3 * 4 * NRBF * BS * BS * 4 * BS * 2 * 3, 10e6),
    )(meta, scalars, vectors, phi, partial, mine, other, own, *weights, *near[1:], tables)


def exchange(x, axis, mask):
    size = lax.axis_size(axis)
    return lax.ppermute(x, axis, [(i, i ^ mask) for i in range(size)])


def gather(x, first=()):
    n_sub = lax.axis_size("sub")
    parts = [None] * n_sub
    for e in range(0, n_sub, 2):
        parts[e] = x if e == 0 else exchange(x, "sub", e)
    if first:
        parts[::2] = lax.optimization_barrier((*parts[::2], *first))[: len(parts[::2])]
    for e in range(0, n_sub, 2):
        parts[e + 1] = exchange(parts[e], "sub", 1)
    return parts


def after(x, *others):
    return lax.optimization_barrier((x, *others))[0]


def body(
    scalars,
    vectors,
    positions,
    pair_blocks,
    pair_mask,
    wavevectors,
    message_in,
    message_out,
    filter_weight,
    ewald_weight,
    ewald_filter,
    mixing_left,
    mixing_right,
    update_in,
    update_out,
):
    n_region = lax.axis_size("region")
    n_sub = lax.axis_size("sub")
    natoms = BS * n_region * n_sub
    scale = 1.0 / math.sqrt(natoms * KW)
    per_region = pair_blocks.shape[1] // n_region
    slots = -(-min(n_sub - 1, per_region) // 2) * 2
    ids = jnp.stack([lax.axis_index("region"), lax.axis_index("sub")]).astype(jnp.int32)
    place = jnp.pad(positions, ((0, 8 - positions.shape[0]), (0, 0)))
    lean = jnp.concatenate([scalars, place], axis=0)
    vectors = vectors.reshape(3 * BS, -1)
    meta = find_pairs(ids, pair_blocks, n_sub, per_region, slots)
    own_trig = own_trig_of(wavevectors, lean)
    tables = region_trig = spots = None
    for layer in range(LAYERS):
        last = layer == LAYERS - 1
        blocks = gather(lean, (meta, own_trig) if layer == 0 else ())
        near = gather(after(vectors, *blocks[2::2]))
        near[0] = vectors
        if layer == 0:
            spots = blocks
            partial, region_trig = structure(layer, blocks, ewald_weight, meta, wavevectors)
        else:
            (partial,) = structure(layer, blocks, ewald_weight, region_trig=region_trig)
        others = [exchange(partial, "region", mask) for mask in range(1, n_region)]
        weights = (message_in, message_out, filter_weight)
        turn = after(meta, partial, *near[2:3])
        if layer == 0:
            along, phi, tables = early_terms(turn, layer, blocks, spots, weights, masks=pair_mask)
        else:
            along, phi = early_terms(turn, layer, blocks, spots, weights, tables=tables)
        *others, along = lax.optimization_barrier((*others, along))
        mine = sum(others, partial)
        theirs = exchange(mine, "sub", 1)
        results = late_terms(
            meta, layer, last, scale, scalars, vectors, phi, near, tables, along, mine, theirs, own_trig,
            (ewald_filter, filter_weight, mixing_left, mixing_right, update_in, update_out),
        )
        if last:
            scalars, vectors = results
        else:
            scalars, vectors = results
            lean = scalars
    return scalars, vectors


def solution(mesh):
    placed = (
        P(("region", "sub"), None),
        P(None, ("region", "sub"), None),
        P(None, ("region", "sub")),
    ) + (P(),) * 12
    return jax.shard_map(
        body,
        mesh=mesh,
        in_specs=placed,
        out_specs=(P(("region", "sub"), None), P(None, ("region", "sub"), None)),
        check_vma=False,
    )
```

```python
import functools
import math

import jax
import jax.numpy as jnp
import numpy as np
from jax import lax
from jax.experimental import pallas as pl
from jax.experimental.pallas import tpu as pltpu
from jax.sharding import PartitionSpec as P

NRBF = 20
BS = 128
KW = 512
LAYERS = 2
BITS = 30
GROUP = 4
CUTOFF = 8.0
SPACING = CUTOFF / (NRBF - 1)
CENTER = 0.5 * CUTOFF
ROOT = math.sqrt(0.5 * math.log2(math.e))
VMEM = 30 * 1024 * 1024
TABLE_SLOTS = 16
WINDOW = 1e10
F32 = jnp.float32
BF16 = jnp.bfloat16


def split(x):
    high = x.astype(BF16)
    return high, (x - high.astype(F32)).astype(BF16)


def wide_left(x):
    high, low = split(x)
    return jnp.concatenate([high, low, high], axis=1)


def wide_right(x):
    high, low = split(x)
    return jnp.concatenate([high, high, low], axis=0)


def stacked(x):
    high, low = split(x)
    return jnp.concatenate([high, high], axis=0), low


def dot(a, b):
    return jnp.dot(a, b, preferred_element_type=F32)


def dot3(a, b):
    return dot(wide_left(a), wide_right(b))


def silu(x):
    return x / (1.0 + jnp.exp(-x))


def turn_fits():
    nodes = 0.5 * np.cos(np.pi * (np.arange(400) + 0.5) / 400)
    cheb = np.polynomial.chebyshev
    fit_cos = cheb.Chebyshev.fit(nodes * nodes, np.cos(2 * np.pi * nodes), 7, domain=[0, 0.25])
    fit_sin = cheb.Chebyshev.fit(nodes * nodes, np.sinc(2 * nodes) * 2 * np.pi, 7, domain=[0, 0.25])
    to_poly = lambda fit: [float(c) for c in fit.convert(kind=np.polynomial.Polynomial).coef]
    return to_poly(fit_cos), to_poly(fit_sin)


COS_FIT, SIN_FIT = turn_fits()


def horner(coefs, x):
    total = jnp.full_like(x, coefs[-1])
    for c in coefs[-2::-1]:
        total = total * x + c
    return total


def cos_sin(turns):
    rest = turns - jnp.round(turns)
    square = rest * rest
    return horner(COS_FIT, square), horner(SIN_FIT, square) * rest


def columns_of(pos):
    return jnp.transpose(pos)


def cost(flops, moved, exps=0):
    return pl.CostEstimate(flops=int(flops), bytes_accessed=int(moved), transcendentals=int(exps))


SMEM_SPEC = pl.BlockSpec(memory_space=pltpu.SMEM)
VMEM_SPEC = pl.BlockSpec(memory_space=pltpu.VMEM)
HBM_SPEC = pl.BlockSpec(memory_space=pltpu.HBM)


def meta_kernel(n_sub, per_region, slots, ids_ref, pairs_ref, meta_ref):
    region, sub = ids_ref[0], ids_ref[1]
    base = region * per_region
    for row in range(5):
        for slot in range(slots):
            meta_ref[row, slot] = lax.rem(sub, 2) if row == 4 else 0

    def visit(p, found):
        first = pairs_ref[0, base + p] - region * n_sub
        second = pairs_ref[1, base + p] - region * n_sub
        hit = (first == sub) | (second == sub)

        @pl.when(hit & (found < slots))
        def _():
            other = jnp.where(first == sub, second, first)
            meta_ref[1, found] = base + p
            meta_ref[2, found] = other ^ sub
            meta_ref[3, found] = (first == sub).astype(jnp.int32)

        return found + hit.astype(jnp.int32)

    meta_ref[0, 0] = lax.fori_loop(0, per_region, visit, jnp.int32(0))


def find_pairs(ids, pair_blocks, n_sub, per_region, slots):
    return pl.pallas_call(
        functools.partial(meta_kernel, n_sub, per_region, slots),
        in_specs=[SMEM_SPEC, SMEM_SPEC],
        out_specs=SMEM_SPEC,
        out_shape=jax.ShapeDtypeStruct((5, slots), jnp.int32),
    )(ids, pair_blocks)


def value_dots(values, sources):
    highs = [v[:, :BS] for v in values]
    both = [b for b, _ in sources]
    low = [l for _, l in sources]
    return dot(jnp.concatenate(values, axis=1), jnp.concatenate(both, axis=0)) + dot(
        jnp.concatenate(highs, axis=1), jnp.concatenate(low, axis=0)
    )


def near_dots(tables, rows, sources):
    return value_dots([tables[i, rows, :] for i in range(len(sources))], sources)


def add_terms(totals, cols, tables, sources, weight):
    total = totals[:, cols]
    for k in range(0, NRBF, GROUP):
        product = near_dots(tables, slice(k * BS, (k + GROUP) * BS), sources)
        total = weigh(total, product, weight, k)
    totals[:, cols] = total


def weigh(total, product, weight, k):
    for g in range(GROUP):
        total = total + product[g * BS : (g + 1) * BS] * weight[k + g : k + g + 1]
    return total


def one_or_two(step, count, act):
    for number in (1, 2):
        here = (2 * step + 1 == count) if number == 1 else (2 * step + 1 < count)
        pl.when(here)(functools.partial(act, number))


def table_copy(table, step, buffer, sems):
    slot = lax.rem(step, 2)
    return pltpu.make_async_copy(table.at[pl.ds(2 * step, 2)], buffer.at[slot], sems.at[slot])


def over_tables(count, table, buffer, sems, act):
    steps = (count + 1) // 2

    def one(step, carry):
        @pl.when(step + 1 < steps)
        def _():
            table_copy(table, step + 1, buffer, sems).start()

        act(step, buffer.at[lax.rem(step, 2)], table_copy(table, step, buffer, sems).wait)
        return carry

    lax.fori_loop(0, steps, one, 0)


def resident_copies(count, table, held, sems):
    steps = (count + 1) // 2
    return [(steps >= back, table_copy(table, steps - back, held, sems)) for back in (1, 2)]


def over_held_tables(count, table, held, buffer, sems, act):
    steps = (count + 1) // 2
    for back in (3, 4):
        pl.when(steps >= back)(table_copy(table, steps - back, buffer, sems).start)

    def resident(at, carry):
        step = steps - 1 - at
        act(step, held.at[lax.rem(step, 2)], lambda: None)
        return carry

    def one(at, carry):
        step = steps - 1 - at
        act(step, buffer.at[lax.rem(step, 2)], table_copy(table, step, buffer, sems).wait)

        @pl.when(step >= 2)
        def _():
            table_copy(table, step - 2, buffer, sems).start()

        return carry

    lax.fori_loop(0, jnp.minimum(steps, 2), resident, 0)
    lax.fori_loop(2, jnp.maximum(steps, 2), one, 0)


def fill_tables(count, tables, act):
    steps = (count + 1) // 2

    def out(step, table, buffer, sems):
        slot = lax.rem(step, 2)
        return pltpu.make_async_copy(buffer.at[slot], table.at[pl.ds(2 * step, 2)], sems.at[slot])

    def one(step, carry):
        @pl.when(step >= 2)
        def _():
            for t in tables:
                out(step - 2, *t).wait()

        act(step, [buffer.at[lax.rem(step, 2)] for _, buffer, _ in tables])
        for t in tables:
            out(step, *t).start()
        return carry

    lax.fori_loop(0, steps, one, 0)
    for back in (2, 1):

        @pl.when(steps >= back)
        def _():
            for t in tables:
                out(steps - back, *t).wait()


def block_views(packed, n_sub):
    chips = n_sub // 2
    height = packed[0].shape[0] // chips
    return [packed[e % 2].at[e // 2 * height : (e // 2 + 1) * height, :] for e in range(n_sub)]


def pair_geometry(meta_ref, listed, near, masks_ref):
    pair = meta_ref[1, listed]
    slot = meta_ref[2, listed]
    is_first = meta_ref[3, listed]
    words = masks_ref[pl.ds(pair, 1), :]
    tiles = -(-words.shape[1] // BS)
    rest = tiles * BS - words.shape[1]
    if rest:
        words = jnp.concatenate([words, jnp.zeros((1, rest), jnp.int32)], axis=1)
    row = lax.broadcasted_iota(jnp.int32, (BS, BS), 0)
    row_tile = (row * 2185) >> 16
    spread = jnp.zeros((BS, BS), jnp.int32)
    for tile in range(tiles):
        spread = jnp.where(
            row_tile == tile,
            jnp.broadcast_to(words[:, tile * BS : (tile + 1) * BS], (BS, BS)),
            spread,
        )
    spot = (row - row_tile * BITS) * BS + lax.broadcasted_iota(jnp.int32, (BS, BS), 1)
    index = (spot * 34953) >> 20
    picked = jnp.take_along_axis(spread, index, axis=1)
    mask = (jnp.right_shift(picked, spot - index * BITS) & 1).astype(F32)
    mask = jnp.where(is_first == 1, mask, jnp.transpose(mask))
    source = jnp.zeros((8, BS), F32)
    for e in range(1, len(near)):
        source = jnp.where(slot == e, near[e][...], source)
    mine = columns_of(near[0][...])
    square = jnp.zeros((BS, BS), F32)
    for d in range(3):
        offset = source[d : d + 1, :] - mine[:, d : d + 1]
        square = square + offset * offset
    distance = jnp.sqrt(square + 1.0)
    inverse = 1.0 / distance
    return jnp.where(mask > 0.5, distance * (ROOT / SPACING), 1.0e4), inverse


def fill_rows(shape, first, at, radial_ref, over_ref):
    scaled, inverse = shape
    kept = []
    for k in range(first, first + GROUP):
        gap = scaled - k * ROOT
        radial = jnp.exp2(-(gap * gap))
        rows = slice(k * BS, (k + 1) * BS)
        for ref, value in ((radial_ref, radial), (over_ref, radial * inverse)):
            high, low = split(value)
            ref[at, rows, 0:BS] = high
            ref[at, rows, BS : 2 * BS] = low
        kept.append(jnp.concatenate([high, low], axis=1))
    return jnp.concatenate(kept, axis=0)


def early_kernel(n_sub, build, layer, meta_ref, *refs):
    blocks = [r.at[:BS, :] for r in block_views(refs[:2], n_sub)]
    places = [r.at[BS:, :] for r in block_views(refs[2:4], n_sub)]
    refs = refs[4:]
    if build:
        in_ref, out_ref, filter_ref, masks_ref, partial_ref, phi_ref, held, tables_hbm = refs[:8]
        sources, totals, over_buffer, over_sems, held_sems = refs[8:]
    else:
        in_ref, out_ref, filter_ref, tables_hbm, partial_ref, phi_ref, held, sources, totals, over_buffer, over_sems, held_sems = refs
    radial_hbm, over_hbm = tables_hbm.at[0], tables_hbm.at[1]
    count = meta_ref[0, 0]
    if not build:

        @pl.when(count > 0)
        def _():
            table_copy(over_hbm, 0, over_buffer, over_sems).start()

        for there, copy in resident_copies(count, radial_hbm, held, held_sems):
            pl.when(there)(copy.start)

    totals[...] = jnp.zeros_like(totals)
    scalars = jnp.concatenate([blocks[e][...] for e in range(1, n_sub)], axis=0)
    hidden = silu(dot3(scalars, in_ref[layer]))
    phi = dot3(hidden, out_ref[layer])
    for e in range(1, n_sub):
        rows = phi[(e - 1) * BS : e * BS]
        phi_ref[e - 1] = rows[:, : 2 * BS]
        phi_r = rows[:, 2 * BS :]
        place = columns_of(places[e][...])
        parts = [phi_r] + [phi_r * (place[:, d : d + 1] - CENTER) for d in range(3)]
        for at, part in enumerate(parts):
            high, low = split(part)
            cols = slice(at * BS, (at + 1) * BS)
            sources[e - 1, 0:BS, cols] = high
            sources[e - 1, BS : 2 * BS, cols] = high
            sources[e - 1, 2 * BS :, cols] = low

    weight = filter_ref[layer, :, 2 * BS :]
    weight = jnp.concatenate([weight, weight], axis=1)

    def near_sources(step, number, tile):
        cols = slice(tile * 2 * BS, (tile + 1) * 2 * BS)
        slots = [meta_ref[2, 2 * step + i] - 1 for i in range(number)]
        return [(sources[e, : 2 * BS, cols], sources[e, 2 * BS :, cols]) for e in slots]

    if build:

        def terms(step, tables, number):
            shapes = [pair_geometry(meta_ref, 2 * step + i, places, masks_ref) for i in range(number)]
            near = [near_sources(step, number, tile) for tile in range(2)]
            both = [totals[:, tile * 2 * BS : (tile + 1) * 2 * BS] for tile in range(2)]
            for k in range(0, NRBF, GROUP):
                over = [fill_rows(shape, k, i, *tables) for i, shape in enumerate(shapes)]
                for tile in range(2):
                    product = value_dots(over, near[tile])
                    both[tile] = weigh(both[tile], product, weight, k)
            for tile in range(2):
                totals[:, tile * 2 * BS : (tile + 1) * 2 * BS] = both[tile]

        def act(step, tables):
            one_or_two(step, count, functools.partial(terms, step, tables))

        fill_tables(
            count, ((radial_hbm, held, held_sems), (over_hbm, over_buffer, over_sems)), act
        )
    else:

        def terms(step, table, ready, number):
            ready()
            for tile in range(2):
                cols = slice(tile * 2 * BS, (tile + 1) * 2 * BS)
                add_terms(totals, cols, table, near_sources(step, number, tile), weight)

        def act(step, table, ready):
            one_or_two(step, count, functools.partial(terms, step, table, ready))

        over_tables(count, over_hbm, over_buffer, over_sems, act)
        for there, copy in resident_copies(count, radial_hbm, held, held_sems):
            pl.when(there)(copy.wait)

    mine = columns_of(places[0][...])
    for d in range(3):
        partial_ref[d * BS : (d + 1) * BS, :] = (
            totals[:, (1 + d) * BS : (2 + d) * BS] - (mine[:, d : d + 1] - CENTER) * totals[:, :BS]
        )


def table_buffers(number):
    return [pltpu.VMEM((2, 2, NRBF * BS, 2 * BS), BF16), pltpu.SemaphoreType.DMA((2,))] * number


def early_terms(meta, layer, n_sub, blocks, spots, weights, masks=None, tables=None):
    slots = meta.shape[1]
    build = tables is None
    shape = jax.ShapeDtypeStruct((2, max(slots, TABLE_SLOTS), NRBF * BS, 2 * BS), BF16)
    out_shape = [
        jax.ShapeDtypeStruct((3 * BS, BS), F32),
        jax.ShapeDtypeStruct((n_sub - 1, BS, 2 * BS), F32),
        jax.ShapeDtypeStruct((2, 2, NRBF * BS, 2 * BS), BF16),
    ]
    return pl.pallas_call(
        functools.partial(early_kernel, n_sub, build, layer),
        in_specs=[SMEM_SPEC] + [VMEM_SPEC] * 7 + [VMEM_SPEC if build else HBM_SPEC],
        out_specs=[VMEM_SPEC] * 3 + ([HBM_SPEC] if build else []),
        scratch_shapes=[
            pltpu.VMEM((n_sub - 1, 3 * BS, 4 * BS), BF16),
            pltpu.VMEM((BS, 4 * BS), F32),
        ]
        + table_buffers(1)
        + [pltpu.SemaphoreType.DMA((2,))],
        out_shape=out_shape + ([shape] if build else []),
        compiler_params=pltpu.CompilerParams(vmem_limit_bytes=VMEM),
        cost_estimate=cost(3 * 4 * NRBF * BS * BS * 4 * BS * 2 * 3, 10e6),
    )(meta, *blocks, *spots, *weights, masks if build else tables)


def own_trig_kernel(waves_ref, place_ref, own_ref):
    waves = waves_ref[...] * (1.0 / (2.0 * math.pi))
    mine = columns_of(place_ref[BS:, :])
    turns = jnp.zeros((BS, waves.shape[1]), F32)
    for d in range(3):
        turns = turns + mine[:, d : d + 1] * waves[d : d + 1, :]
    own_ref[...] = jnp.concatenate(split(jnp.concatenate(cos_sin(turns), axis=1)), axis=1)


def own_trig_of(waves, spot):
    return pl.pallas_call(
        own_trig_kernel,
        in_specs=[VMEM_SPEC] * 2,
        out_specs=VMEM_SPEC,
        out_shape=jax.ShapeDtypeStruct((BS, 4 * KW), BF16),
        compiler_params=pltpu.CompilerParams(vmem_limit_bytes=VMEM),
        cost_estimate=cost(WINDOW, 1e6),
    )(waves, spot)


def structure_kernel(n_sub, build, layer, *refs):
    if build:
        meta_ref, waves_ref, refs = refs[0], refs[1], refs[2:]
        places = [r.at[BS:, :] for r in block_views(refs[:2], n_sub)]
    blocks, refs = [r.at[:BS, :] for r in block_views(refs[:2], n_sub)], refs[2:]
    atoms = n_sub * BS
    if build:
        weight_ref, out_ref, trig_ref = refs
        waves = waves_ref[...] * (1.0 / (2.0 * math.pi))
        rows = waves.shape[1] // 2
        waves = jnp.where(meta_ref[4, 0] == 0, waves[:, :rows], waves[:, rows:])
        half = jnp.transpose(jnp.concatenate([waves, jnp.zeros((5, rows), F32)], axis=0))
        for e in range(n_sub):
            place = places[e][...]
            turns = jnp.zeros((rows, BS), F32)
            for d in range(3):
                turns = turns + half[:, d : d + 1] * place[d : d + 1, :]
            for at, value in enumerate(cos_sin(turns)):
                block = slice(at * rows, (at + 1) * rows)
                for part, piece in enumerate(split(value)):
                    trig_ref[block, part * atoms + e * BS : part * atoms + (e + 1) * BS] = piece
    else:
        weight_ref, trig_ref, out_ref = refs
    both, low = stacked(jnp.concatenate([blocks[e][...] for e in range(n_sub)], axis=0))
    total = dot(trig_ref[...], both) + dot(trig_ref[:, :atoms], low)
    out_ref[...] = dot3(total, weight_ref[layer])


def structure(layer, n_sub, blocks, weight, meta=None, waves=None, region_trig=None):
    build = region_trig is None
    out_shape = [jax.ShapeDtypeStruct((KW, BS), F32)]
    if build:
        in_specs = [SMEM_SPEC] + [VMEM_SPEC] * 4
        operands = (meta, waves, *blocks, weight)
        out_shape += [jax.ShapeDtypeStruct((KW, 2 * n_sub * BS), BF16)]
    else:
        in_specs = [VMEM_SPEC] * 4
        operands = (*blocks, weight, region_trig)
    return pl.pallas_call(
        functools.partial(structure_kernel, n_sub, build, layer),
        in_specs=in_specs,
        out_specs=[VMEM_SPEC] * len(out_shape),
        out_shape=out_shape,
        compiler_params=pltpu.CompilerParams(vmem_limit_bytes=VMEM),
        cost_estimate=cost(KW * n_sub * BS * BS * 6, 4e6),
    )(*operands)


def late_kernel(n_sub, layer, meta_ref, *refs):
    phi_ref, partial_ref, filter_ref = refs[:3]
    near, refs = refs[3 : 2 + n_sub], refs[2 + n_sub :]
    tables_hbm, held, totals, buffer, sems = refs
    radial_hbm = tables_hbm.at[0]
    count = meta_ref[0, 0]

    totals[:, :BS] = jnp.zeros((BS, BS), F32)
    for d in range(3):
        totals[:, (1 + d) * BS : (2 + d) * BS] = partial_ref[d * BS : (d + 1) * BS, :]
    w_s, w_v = filter_ref[layer, :, :BS], filter_ref[layer, :, BS : 2 * BS]

    def terms(step, table, ready, number):
        parts = []
        for i in range(number):
            slot = meta_ref[2, 2 * step + i]
            vectors = near[0][...]
            for e in range(2, n_sub):
                vectors = jnp.where(slot == e, near[e - 1][...], vectors)
            phi = phi_ref[slot - 1]
            phi_s, phi_v = phi[:, :BS], phi[:, BS:]
            parts.append([phi_s] + [phi_v * vectors[d * BS : (d + 1) * BS, :] for d in range(3)])
        sources = [
            [stacked(jnp.concatenate(p[2 * tile : 2 * tile + 2], axis=1)) for p in parts] for tile in range(2)
        ]
        ready()
        for tile, names in enumerate(((w_s, w_v), (w_v, w_v))):
            cols = slice(tile * 2 * BS, (tile + 1) * 2 * BS)
            add_terms(totals, cols, table, sources[tile], jnp.concatenate(names, axis=1))

    def act(step, table, ready):
        one_or_two(step, count, functools.partial(terms, step, table, ready))

    over_held_tables(count, radial_hbm, held, buffer, sems, act)


def late_terms(meta, layer, phi, near, tables, held, partial, weight):
    n_sub = len(near)
    return pl.pallas_call(
        functools.partial(late_kernel, n_sub, layer),
        in_specs=[SMEM_SPEC] + [VMEM_SPEC] * (2 + n_sub) + [HBM_SPEC, VMEM_SPEC],
        out_specs=VMEM_SPEC,
        scratch_shapes=table_buffers(1),
        out_shape=jax.ShapeDtypeStruct((BS, 4 * BS), F32),
        compiler_params=pltpu.CompilerParams(vmem_limit_bytes=VMEM),
        cost_estimate=cost(3 * 4 * NRBF * BS * BS * 4 * BS * 2 * 3, 10e6),
    )(meta, phi, partial, weight, *near[1:], tables, held)


def update_kernel(scale, layer, last, meta_ref, *refs):
    scalars_ref, vectors_ref, totals, mine_ref, other_ref, own_ref = refs[:6]
    factor_ref, left_ref, right_ref, gate_in_ref, gate_out_ref = refs[6:11]
    outs = refs[11:]
    lower = meta_ref[4, 0] == 0
    mine, other = mine_ref[...], other_ref[...]
    half = mine.shape[0] // 2
    first = jnp.where(lower, mine, other)
    second = jnp.where(lower, other, mine)
    factors = factor_ref[layer] * scale
    both, low = stacked(
        jnp.concatenate(
            [
                first[:half] * factors[:half],
                second[:half] * factors[half:],
                first[half:] * factors[:half],
                second[half:] * factors[half:],
            ],
            axis=0,
        )
    )
    ewald = dot(own_ref[...], both) + dot(own_ref[:, : 2 * KW], low)
    mid_scalars = scalars_ref[...] + totals[:, :BS] + ewald
    mid_vectors = jnp.concatenate(
        [vectors_ref[d * BS : (d + 1) * BS, :] + totals[:, (1 + d) * BS : (2 + d) * BS] for d in range(3)], axis=0
    )
    mixed = dot3(mid_vectors, jnp.concatenate([left_ref[layer], right_ref[layer]], axis=1))
    left, right = mixed[:, :BS], mixed[:, BS:]
    parts = [slice(d * BS, (d + 1) * BS) for d in range(3)]
    norm = jnp.sqrt(sum(right[p] * right[p] for p in parts) + 1.0)
    along = sum(left[p] * right[p] for p in parts)
    hidden = silu(dot3(jnp.concatenate([mid_scalars, norm], axis=1), gate_in_ref[layer]))
    gates = dot3(hidden, gate_out_ref[layer])
    g_v, g_sv, g_s = (gates[:, i * BS : (i + 1) * BS] for i in range(3))
    new_scalars = mid_scalars + g_sv * along + g_s
    new_vectors = [mid_vectors[p] + g_v * left[p] for p in parts]
    if last:
        outs[0][...] = new_scalars
        for d in range(3):
            outs[1][d] = new_vectors[d]
    else:
        outs[0][...] = new_scalars
        for d, p in enumerate(parts):
            outs[1][p, :] = new_vectors[d]


def update(meta, layer, last, scale, scalars, vectors, totals, mine, other, own, weights):
    shapes = [(BS, BS), (3, BS, BS)] if last else [(BS, BS), (3 * BS, BS)]
    return pl.pallas_call(
        functools.partial(update_kernel, scale, layer, last),
        in_specs=[SMEM_SPEC] + [VMEM_SPEC] * 11,
        out_specs=[VMEM_SPEC] * len(shapes),
        out_shape=[jax.ShapeDtypeStruct(shape, F32) for shape in shapes],
        compiler_params=pltpu.CompilerParams(vmem_limit_bytes=VMEM),
        cost_estimate=cost(3e9, 4e6),
    )(meta, scalars, vectors, totals, mine, other, own, *weights)


def exchange(x, axis, mask):
    size = lax.axis_size(axis)
    return lax.ppermute(x, axis, [(i, i ^ mask) for i in range(size)])


def from_chips(x):
    return [x] + [exchange(x, "sub", e) for e in range(2, lax.axis_size("sub"), 2)]


def both_cores(parts):
    return [p for pair in zip(parts, [exchange(p, "sub", 1) for p in parts]) for p in pair]


def after(x, *others):
    return lax.optimization_barrier((x, *others))[0]


def body(
    scalars,
    vectors,
    positions,
    pair_blocks,
    pair_mask,
    wavevectors,
    message_in,
    message_out,
    filter_weight,
    ewald_weight,
    ewald_filter,
    mixing_left,
    mixing_right,
    update_in,
    update_out,
):
    n_region = lax.axis_size("region")
    n_sub = lax.axis_size("sub")
    natoms = BS * n_region * n_sub
    scale = 1.0 / math.sqrt(natoms * KW)
    per_region = pair_blocks.shape[1] // n_region
    slots = -(-min(n_sub - 1, per_region) // 2) * 2
    ids = jnp.stack([lax.axis_index("region"), lax.axis_index("sub")]).astype(jnp.int32)
    place = jnp.pad(positions, ((0, 8 - positions.shape[0]), (0, 0)))
    lean = jnp.concatenate([scalars, place], axis=0)
    vectors = vectors.reshape(3 * BS, -1)
    meta = find_pairs(ids, pair_blocks, n_sub, per_region, slots)
    own_trig = own_trig_of(wavevectors, lean)
    tables = region_trig = spots = None
    for layer in range(LAYERS):
        last = layer == LAYERS - 1
        scalar_parts = from_chips(lean)
        if layer == 0:
            scalar_parts = lax.optimization_barrier((*scalar_parts, meta, own_trig))[:-2]
        packed = jnp.concatenate(scalar_parts, axis=0)
        blocks = (packed, exchange(packed, "sub", 1))
        vector_parts = from_chips(after(vectors, scalar_parts[1]))
        near = both_cores(vector_parts)
        if layer == 0:
            spots = blocks
            partial, region_trig = structure(layer, n_sub, blocks, ewald_weight, meta, wavevectors)
        else:
            (partial,) = structure(layer, n_sub, blocks, ewald_weight, region_trig=region_trig)
        others = [exchange(partial, "region", mask) for mask in range(1, n_region)]
        weights = (message_in, message_out, filter_weight)
        turn = after(meta, partial, *near[2:3])
        if layer == 0:
            along, phi, held, tables = early_terms(turn, layer, n_sub, blocks, spots, weights, masks=pair_mask)
        else:
            along, phi, held = early_terms(turn, layer, n_sub, blocks, spots, weights, tables=tables)
        others = lax.optimization_barrier((*others, along))[:-1]
        mine = sum(others, partial)
        theirs = exchange(mine, "sub", 1)
        totals = late_terms(meta, layer, phi, near, tables, held, along, filter_weight)
        results = update(
            meta, layer, last, scale, scalars, vectors, totals, mine, theirs, own_trig,
            (ewald_filter, mixing_left, mixing_right, update_in, update_out),
        )
        scalars, vectors = results
        lean = scalars
    return scalars, vectors


def solution(mesh):
    placed = (
        P(("region", "sub"), None),
        P(None, ("region", "sub"), None),
        P(None, ("region", "sub")),
    ) + (P(),) * 12
    return jax.shard_map(
        body,
        mesh=mesh,
        in_specs=placed,
        out_specs=(P(("region", "sub"), None), P(None, ("region", "sub"), None)),
        check_vma=False,
    )
```

```python
import functools
import math

import jax
import jax.numpy as jnp
import numpy as np
from jax import lax
from jax.experimental import pallas as pl
from jax.experimental.pallas import tpu as pltpu
from jax.sharding import PartitionSpec as P

NRBF = 20
BS = 128
KW = 512
LAYERS = 2
BITS = 30
GROUP = 4
CUTOFF = 8.0
SPACING = CUTOFF / (NRBF - 1)
CENTER = 0.5 * CUTOFF
ROOT = math.sqrt(0.5 * math.log2(math.e))
VMEM = 30 * 1024 * 1024
TABLE_SLOTS = 16
WINDOW = 1e10
F32 = jnp.float32
BF16 = jnp.bfloat16


def split(x):
    high = x.astype(BF16)
    return high, (x - high.astype(F32)).astype(BF16)


def wide_left(x):
    high, low = split(x)
    return jnp.concatenate([high, low, high], axis=1)


def wide_right(x):
    high, low = split(x)
    return jnp.concatenate([high, high, low], axis=0)


def stacked(x):
    high, low = split(x)
    return jnp.concatenate([high, high], axis=0), low


def dot(a, b):
    return jnp.dot(a, b, preferred_element_type=F32)


def dot3(a, b):
    return dot(wide_left(a), wide_right(b))


def silu(x):
    return x / (1.0 + jnp.exp(-x))


def turn_fits():
    nodes = 0.5 * np.cos(np.pi * (np.arange(400) + 0.5) / 400)
    cheb = np.polynomial.chebyshev
    fit_cos = cheb.Chebyshev.fit(nodes * nodes, np.cos(2 * np.pi * nodes), 7, domain=[0, 0.25])
    fit_sin = cheb.Chebyshev.fit(nodes * nodes, np.sinc(2 * nodes) * 2 * np.pi, 7, domain=[0, 0.25])
    to_poly = lambda fit: [float(c) for c in fit.convert(kind=np.polynomial.Polynomial).coef]
    return to_poly(fit_cos), to_poly(fit_sin)


COS_FIT, SIN_FIT = turn_fits()


def horner(coefs, x):
    total = jnp.full_like(x, coefs[-1])
    for c in coefs[-2::-1]:
        total = total * x + c
    return total


def cos_sin(turns):
    rest = turns - jnp.round(turns)
    square = rest * rest
    return horner(COS_FIT, square), horner(SIN_FIT, square) * rest


def columns_of(pos):
    return jnp.transpose(pos)


def cost(flops, moved, exps=0):
    return pl.CostEstimate(flops=int(flops), bytes_accessed=int(moved), transcendentals=int(exps))


SMEM_SPEC = pl.BlockSpec(memory_space=pltpu.SMEM)
VMEM_SPEC = pl.BlockSpec(memory_space=pltpu.VMEM)
HBM_SPEC = pl.BlockSpec(memory_space=pltpu.HBM)


def meta_kernel(n_sub, per_region, slots, ids_ref, pairs_ref, meta_ref):
    region, sub = ids_ref[0], ids_ref[1]
    base = region * per_region
    for row in range(6):
        for slot in range(slots):
            meta_ref[row, slot] = lax.rem(sub, 2) if row == 4 else 0

    def visit(p, found):
        first = pairs_ref[0, base + p] - region * n_sub
        second = pairs_ref[1, base + p] - region * n_sub
        hit = (first == sub) | (second == sub)

        @pl.when(hit & (found < slots))
        def _():
            other = jnp.where(first == sub, second, first)
            meta_ref[1, found] = base + p
            meta_ref[2, found] = other ^ sub
            meta_ref[3, found] = (first == sub).astype(jnp.int32)
            meta_ref[5, found] = near_place(other ^ sub, lax.rem(sub, 2))

        return found + hit.astype(jnp.int32)

    meta_ref[0, 0] = lax.fori_loop(0, per_region, visit, jnp.int32(0))


def find_pairs(ids, pair_blocks, n_sub, per_region, slots):
    return pl.pallas_call(
        functools.partial(meta_kernel, n_sub, per_region, slots),
        in_specs=[SMEM_SPEC, SMEM_SPEC],
        out_specs=SMEM_SPEC,
        out_shape=jax.ShapeDtypeStruct((6, slots), jnp.int32),
    )(ids, pair_blocks)


def value_dots(values, sources):
    highs = [v[:, :BS] for v in values]
    both = [b for b, _ in sources]
    low = [l for _, l in sources]
    return dot(jnp.concatenate(values, axis=1), jnp.concatenate(both, axis=0)) + dot(
        jnp.concatenate(highs, axis=1), jnp.concatenate(low, axis=0)
    )


def near_dots(tables, rows, sources):
    return value_dots([tables[i, rows, :] for i in range(len(sources))], sources)


def add_terms(totals, cols, tables, sources, weight):
    total = totals[:, cols]
    for k in range(0, NRBF, GROUP):
        product = near_dots(tables, slice(k * BS, (k + GROUP) * BS), sources)
        total = weigh(total, product, weight, k)
    totals[:, cols] = total


def weigh(total, product, weight, k):
    for g in range(GROUP):
        total = total + product[g * BS : (g + 1) * BS] * weight[k + g : k + g + 1]
    return total


def one_or_two(step, count, act):
    for number in (1, 2):
        here = (2 * step + 1 == count) if number == 1 else (2 * step + 1 < count)
        pl.when(here)(functools.partial(act, number))


def table_copy(table, step, buffer, sems):
    slot = lax.rem(step, 2)
    return pltpu.make_async_copy(table.at[pl.ds(2 * step, 2)], buffer.at[slot], sems.at[slot])


def over_tables(count, table, held, buffer, sems, act):
    steps = (count + 1) // 2
    for back in (3, 4):
        pl.when(steps >= back)(table_copy(table, steps - back, buffer, sems).start)

    def resident(at, carry):
        step = steps - 1 - at
        act(step, held.at[lax.rem(step, 2)], lambda: None)
        return carry

    def one(at, carry):
        step = steps - 1 - at
        act(step, buffer.at[lax.rem(step, 2)], table_copy(table, step, buffer, sems).wait)

        @pl.when(step >= 2)
        def _():
            table_copy(table, step - 2, buffer, sems).start()

        return carry

    lax.fori_loop(0, jnp.minimum(steps, 2), resident, 0)
    lax.fori_loop(2, jnp.maximum(steps, 2), one, 0)


def fill_tables(count, tables, act):
    steps = (count + 1) // 2

    def out(step, table, buffer, sems):
        slot = lax.rem(step, 2)
        return pltpu.make_async_copy(buffer.at[slot], table.at[pl.ds(2 * step, 2)], sems.at[slot])

    def one(step, carry):
        @pl.when(step >= 2)
        def _():
            for t in tables:
                out(step - 2, *t).wait()

        act(step, [buffer.at[lax.rem(step, 2)] for _, buffer, _ in tables])
        for t in tables:
            out(step, *t).start()
        return carry

    lax.fori_loop(0, steps, one, 0)
    for back in (2, 1):

        @pl.when(steps >= back)
        def _():
            for t in tables:
                out(steps - back, *t).wait()


def block_views(packed, n_sub):
    chips = n_sub // 2
    height = packed[0].shape[0] // chips
    return [packed[e % 2].at[e // 2 * height : (e // 2 + 1) * height, :] for e in range(n_sub)]


def pair_geometry(meta_ref, listed, near, masks_ref):
    pair = meta_ref[1, listed]
    slot = meta_ref[2, listed]
    is_first = meta_ref[3, listed]
    words = masks_ref[pl.ds(pair, 1), :]
    tiles = -(-words.shape[1] // BS)
    rest = tiles * BS - words.shape[1]
    if rest:
        words = jnp.concatenate([words, jnp.zeros((1, rest), jnp.int32)], axis=1)
    row = lax.broadcasted_iota(jnp.int32, (BS, BS), 0)
    row_tile = (row * 2185) >> 16
    spread = jnp.zeros((BS, BS), jnp.int32)
    for tile in range(tiles):
        spread = jnp.where(
            row_tile == tile,
            jnp.broadcast_to(words[:, tile * BS : (tile + 1) * BS], (BS, BS)),
            spread,
        )
    spot = (row - row_tile * BITS) * BS + lax.broadcasted_iota(jnp.int32, (BS, BS), 1)
    index = (spot * 34953) >> 20
    picked = jnp.take_along_axis(spread, index, axis=1)
    mask = (jnp.right_shift(picked, spot - index * BITS) & 1).astype(F32)
    mask = jnp.where(is_first == 1, mask, jnp.transpose(mask))
    source = jnp.zeros((8, BS), F32)
    for e in range(1, len(near)):
        source = jnp.where(slot == e, near[e][...], source)
    mine = columns_of(near[0][...])
    square = jnp.zeros((BS, BS), F32)
    for d in range(3):
        offset = source[d : d + 1, :] - mine[:, d : d + 1]
        square = square + offset * offset
    distance = jnp.sqrt(square + 1.0)
    inverse = 1.0 / distance
    return jnp.where(mask > 0.5, distance * (ROOT / SPACING), 1.0e4), inverse


def fill_rows(shape, first, at, radial_ref, over_ref):
    scaled, inverse = shape
    kept = []
    for k in range(first, first + GROUP):
        gap = scaled - k * ROOT
        radial = jnp.exp2(-(gap * gap))
        rows = slice(k * BS, (k + 1) * BS)
        for ref, value in ((radial_ref, radial), (over_ref, radial * inverse)):
            high, low = split(value)
            ref[at, rows, 0:BS] = high
            ref[at, rows, BS : 2 * BS] = low
        kept.append(jnp.concatenate([high, low], axis=1))
    return jnp.concatenate(kept, axis=0)


def early_kernel(n_sub, build, layer, meta_ref, *refs):
    blocks = [r.at[:BS, :] for r in block_views(refs[:2], n_sub)]
    places = [r.at[BS:, :] for r in block_views(refs[2:4], n_sub)]
    refs = refs[4:]
    if build:
        in_ref, out_ref, filter_ref, masks_ref, partial_ref, phi_ref, held, held_over, tables_hbm = refs[:9]
        sources, totals, held_sems, over_sems = refs[9:]
    else:
        in_ref, out_ref, filter_ref, tables_hbm, held_over, partial_ref, phi_ref, sources, totals, buffer, sems = refs
    radial_hbm, over_hbm = tables_hbm.at[0], tables_hbm.at[1]
    count = meta_ref[0, 0]
    totals[...] = jnp.zeros_like(totals)
    scalars = jnp.concatenate([blocks[e][...] for e in range(1, n_sub)], axis=0)
    hidden = silu(dot3(scalars, in_ref[layer]))
    phi = dot3(hidden, out_ref[layer])
    for e in range(1, n_sub):
        rows = phi[(e - 1) * BS : e * BS]
        phi_ref[e - 1] = rows[:, : 2 * BS]
        phi_r = rows[:, 2 * BS :]
        place = columns_of(places[e][...])
        parts = [phi_r] + [phi_r * (place[:, d : d + 1] - CENTER) for d in range(3)]
        for at, part in enumerate(parts):
            high, low = split(part)
            cols = slice(at * BS, (at + 1) * BS)
            sources[e - 1, 0:BS, cols] = high
            sources[e - 1, BS : 2 * BS, cols] = high
            sources[e - 1, 2 * BS :, cols] = low

    weight = filter_ref[layer, :, 2 * BS :]
    weight = jnp.concatenate([weight, weight], axis=1)

    def near_sources(step, number, tile):
        cols = slice(tile * 2 * BS, (tile + 1) * 2 * BS)
        slots = [meta_ref[2, 2 * step + i] - 1 for i in range(number)]
        return [(sources[e, : 2 * BS, cols], sources[e, 2 * BS :, cols]) for e in slots]

    if build:

        def terms(step, tables, number):
            shapes = [pair_geometry(meta_ref, 2 * step + i, places, masks_ref) for i in range(number)]
            near = [near_sources(step, number, tile) for tile in range(2)]
            both = [totals[:, tile * 2 * BS : (tile + 1) * 2 * BS] for tile in range(2)]
            for k in range(0, NRBF, GROUP):
                over = [fill_rows(shape, k, i, *tables) for i, shape in enumerate(shapes)]
                for tile in range(2):
                    product = value_dots(over, near[tile])
                    both[tile] = weigh(both[tile], product, weight, k)
            for tile in range(2):
                totals[:, tile * 2 * BS : (tile + 1) * 2 * BS] = both[tile]

        def act(step, tables):
            one_or_two(step, count, functools.partial(terms, step, tables))

        fill_tables(
            count, ((radial_hbm, held, held_sems), (over_hbm, held_over, over_sems)), act
        )
    else:

        def terms(step, table, ready, number):
            ready()
            for tile in range(2):
                cols = slice(tile * 2 * BS, (tile + 1) * 2 * BS)
                add_terms(totals, cols, table, near_sources(step, number, tile), weight)

        def act(step, table, ready):
            one_or_two(step, count, functools.partial(terms, step, table, ready))

        over_tables(count, over_hbm, held_over, buffer, sems, act)

    mine = columns_of(places[0][...])
    for d in range(3):
        partial_ref[d * BS : (d + 1) * BS, :] = (
            totals[:, (1 + d) * BS : (2 + d) * BS] - (mine[:, d : d + 1] - CENTER) * totals[:, :BS]
        )


def table_buffers(number):
    return [pltpu.VMEM((2, 2, NRBF * BS, 2 * BS), BF16), pltpu.SemaphoreType.DMA((2,))] * number


def early_terms(meta, layer, n_sub, blocks, spots, weights, masks=None, tables=None, held=None):
    slots = meta.shape[1]
    build = tables is None
    out_shape = [
        jax.ShapeDtypeStruct((3 * BS, BS), F32),
        jax.ShapeDtypeStruct((n_sub - 1, BS, 2 * BS), F32),
    ]
    two = jax.ShapeDtypeStruct((2, 2, NRBF * BS, 2 * BS), BF16)
    every = jax.ShapeDtypeStruct((2, max(slots, TABLE_SLOTS), NRBF * BS, 2 * BS), BF16)
    return pl.pallas_call(
        functools.partial(early_kernel, n_sub, build, layer),
        in_specs=[SMEM_SPEC] + [VMEM_SPEC] * 7 + ([VMEM_SPEC] if build else [HBM_SPEC, VMEM_SPEC]),
        out_specs=[VMEM_SPEC] * 2 + ([VMEM_SPEC] * 2 + [HBM_SPEC] if build else []),
        scratch_shapes=[
            pltpu.VMEM((n_sub - 1, 3 * BS, 4 * BS), BF16),
            pltpu.VMEM((BS, 4 * BS), F32),
        ]
        + ([pltpu.SemaphoreType.DMA((2,))] * 2 if build else table_buffers(1)),
        out_shape=out_shape + ([two, two, every] if build else []),
        compiler_params=pltpu.CompilerParams(vmem_limit_bytes=VMEM),
        cost_estimate=cost(3 * 4 * NRBF * BS * BS * 4 * BS * 2 * 3, 10e6),
    )(meta, *blocks, *spots, *weights, *((masks,) if build else (tables, held)))


def own_trig_kernel(waves_ref, place_ref, own_ref):
    waves = waves_ref[...] * (1.0 / (2.0 * math.pi))
    mine = columns_of(place_ref[BS:, :])
    turns = jnp.zeros((BS, waves.shape[1]), F32)
    for d in range(3):
        turns = turns + mine[:, d : d + 1] * waves[d : d + 1, :]
    own_ref[...] = jnp.concatenate(split(jnp.concatenate(cos_sin(turns), axis=1)), axis=1)


def own_trig_of(waves, spot):
    return pl.pallas_call(
        own_trig_kernel,
        in_specs=[VMEM_SPEC] * 2,
        out_specs=VMEM_SPEC,
        out_shape=jax.ShapeDtypeStruct((BS, 4 * KW), BF16),
        compiler_params=pltpu.CompilerParams(vmem_limit_bytes=VMEM),
        cost_estimate=cost(WINDOW, 1e6),
    )(waves, spot)


def structure_kernel(n_sub, build, layer, *refs):
    if build:
        meta_ref, waves_ref, refs = refs[0], refs[1], refs[2:]
        places = [r.at[BS:, :] for r in block_views(refs[:2], n_sub)]
    blocks, refs = [r.at[:BS, :] for r in block_views(refs[:2], n_sub)], refs[2:]
    atoms = n_sub * BS
    if build:
        weight_ref, out_ref, trig_ref = refs
        waves = waves_ref[...] * (1.0 / (2.0 * math.pi))
        rows = waves.shape[1] // 2
        waves = jnp.where(meta_ref[4, 0] == 0, waves[:, :rows], waves[:, rows:])
        half = jnp.transpose(jnp.concatenate([waves, jnp.zeros((5, rows), F32)], axis=0))
        for e in range(n_sub):
            place = places[e][...]
            turns = jnp.zeros((rows, BS), F32)
            for d in range(3):
                turns = turns + half[:, d : d + 1] * place[d : d + 1, :]
            for at, value in enumerate(cos_sin(turns)):
                block = slice(at * rows, (at + 1) * rows)
                for part, piece in enumerate(split(value)):
                    trig_ref[block, part * atoms + e * BS : part * atoms + (e + 1) * BS] = piece
    else:
        weight_ref, trig_ref, out_ref = refs
    both, low = stacked(jnp.concatenate([blocks[e][...] for e in range(n_sub)], axis=0))
    total = dot(trig_ref[...], both) + dot(trig_ref[:, :atoms], low)
    out_ref[...] = dot3(total, weight_ref[layer])


def structure(layer, n_sub, blocks, weight, meta=None, waves=None, region_trig=None):
    build = region_trig is None
    out_shape = [jax.ShapeDtypeStruct((KW, BS), F32)]
    if build:
        in_specs = [SMEM_SPEC] + [VMEM_SPEC] * 4
        operands = (meta, waves, *blocks, weight)
        out_shape += [jax.ShapeDtypeStruct((KW, 2 * n_sub * BS), BF16)]
    else:
        in_specs = [VMEM_SPEC] * 4
        operands = (*blocks, weight, region_trig)
    return pl.pallas_call(
        functools.partial(structure_kernel, n_sub, build, layer),
        in_specs=in_specs,
        out_specs=[VMEM_SPEC] * len(out_shape),
        out_shape=out_shape,
        compiler_params=pltpu.CompilerParams(vmem_limit_bytes=VMEM),
        cost_estimate=cost(KW * n_sub * BS * BS * 6, 4e6),
    )(*operands)


def late_kernel(arrays, layer, paired, meta_ref, *refs):
    phi_ref, partial_ref, filter_ref = refs[:3]
    near, refs = refs[3 : 3 + arrays], refs[3 + arrays :]
    near = [r.at[at : at + 3 * BS, :] for r in near for at in range(0, r.shape[0], 3 * BS)]
    tables_hbm, held, totals, buffer, sems = refs
    radial_hbm = tables_hbm.at[0]
    count = meta_ref[0, 0]

    totals[:, :BS] = jnp.zeros((BS, BS), F32)
    for d in range(3):
        totals[:, (1 + d) * BS : (2 + d) * BS] = partial_ref[d * BS : (d + 1) * BS, :]
    w_s, w_v = filter_ref[layer, :, :BS], filter_ref[layer, :, BS : 2 * BS]

    def terms(step, table, ready, number):
        parts = []
        for i in range(number):
            slot = meta_ref[2, 2 * step + i]
            place = meta_ref[5, 2 * step + i] if paired else slot - 1
            vectors = near[0][...]
            for at in range(1, len(near)):
                vectors = jnp.where(place == at, near[at][...], vectors)
            phi = phi_ref[slot - 1]
            phi_s, phi_v = phi[:, :BS], phi[:, BS:]
            parts.append([phi_s] + [phi_v * vectors[d * BS : (d + 1) * BS, :] for d in range(3)])
        sources = [
            [stacked(jnp.concatenate(p[2 * tile : 2 * tile + 2], axis=1)) for p in parts] for tile in range(2)
        ]
        ready()
        for tile, names in enumerate(((w_s, w_v), (w_v, w_v))):
            cols = slice(tile * 2 * BS, (tile + 1) * 2 * BS)
            add_terms(totals, cols, table, sources[tile], jnp.concatenate(names, axis=1))

    def act(step, table, ready):
        one_or_two(step, count, functools.partial(terms, step, table, ready))

    over_tables(count, radial_hbm, held, buffer, sems, act)


def late_terms(meta, layer, paired, phi, near, tables, held, partial, weight):
    arrays = len(near)
    return pl.pallas_call(
        functools.partial(late_kernel, arrays, layer, paired),
        in_specs=[SMEM_SPEC] + [VMEM_SPEC] * (3 + arrays) + [HBM_SPEC, VMEM_SPEC],
        out_specs=VMEM_SPEC,
        scratch_shapes=table_buffers(1),
        out_shape=jax.ShapeDtypeStruct((BS, 4 * BS), F32),
        compiler_params=pltpu.CompilerParams(vmem_limit_bytes=VMEM),
        cost_estimate=cost(3 * 4 * NRBF * BS * BS * 4 * BS * 2 * 3, 10e6),
    )(meta, phi, partial, weight, *near, tables, held)


def update_kernel(scale, layer, last, meta_ref, *refs):
    scalars_ref, vectors_ref, totals, mine_ref, other_ref, own_ref = refs[:6]
    factor_ref, left_ref, right_ref, gate_in_ref, gate_out_ref = refs[6:11]
    outs = refs[11:]
    lower = meta_ref[4, 0] == 0
    mine, other = mine_ref[...], other_ref[...]
    half = mine.shape[0] // 2
    first = jnp.where(lower, mine, other)
    second = jnp.where(lower, other, mine)
    factors = factor_ref[layer] * scale
    both, low = stacked(
        jnp.concatenate(
            [
                first[:half] * factors[:half],
                second[:half] * factors[half:],
                first[half:] * factors[:half],
                second[half:] * factors[half:],
            ],
            axis=0,
        )
    )
    ewald = dot(own_ref[...], both) + dot(own_ref[:, : 2 * KW], low)
    mid_scalars = scalars_ref[...] + totals[:, :BS] + ewald
    mid_vectors = jnp.concatenate(
        [vectors_ref[d * BS : (d + 1) * BS, :] + totals[:, (1 + d) * BS : (2 + d) * BS] for d in range(3)], axis=0
    )
    mixed = dot3(mid_vectors, jnp.concatenate([left_ref[layer], right_ref[layer]], axis=1))
    left, right = mixed[:, :BS], mixed[:, BS:]
    parts = [slice(d * BS, (d + 1) * BS) for d in range(3)]
    norm = jnp.sqrt(sum(right[p] * right[p] for p in parts) + 1.0)
    along = sum(left[p] * right[p] for p in parts)
    hidden = silu(dot3(jnp.concatenate([mid_scalars, norm], axis=1), gate_in_ref[layer]))
    gates = dot3(hidden, gate_out_ref[layer])
    g_v, g_sv, g_s = (gates[:, i * BS : (i + 1) * BS] for i in range(3))
    new_scalars = mid_scalars + g_sv * along + g_s
    new_vectors = [mid_vectors[p] + g_v * left[p] for p in parts]
    if last:
        outs[0][...] = new_scalars
        for d in range(3):
            outs[1][d] = new_vectors[d]
    else:
        outs[0][...] = new_scalars
        for d, p in enumerate(parts):
            outs[1][p, :] = new_vectors[d]


def update(meta, layer, last, scale, scalars, vectors, totals, mine, other, own, weights):
    shapes = [(BS, BS), (3, BS, BS)] if last else [(BS, BS), (3 * BS, BS)]
    return pl.pallas_call(
        functools.partial(update_kernel, scale, layer, last),
        in_specs=[SMEM_SPEC] + [VMEM_SPEC] * 11,
        out_specs=[VMEM_SPEC] * len(shapes),
        out_shape=[jax.ShapeDtypeStruct(shape, F32) for shape in shapes],
        compiler_params=pltpu.CompilerParams(vmem_limit_bytes=VMEM),
        cost_estimate=cost(3e9, 4e6),
    )(meta, scalars, vectors, totals, mine, other, own, *weights)


def exchange(x, axis, mask):
    size = lax.axis_size(axis)
    return lax.ppermute(x, axis, [(i, i ^ mask) for i in range(size)])


def from_chips(x):
    return [x] + [exchange(x, "sub", e) for e in range(2, lax.axis_size("sub"), 2)]


def both_cores(parts):
    return [p for pair in zip(parts, [exchange(p, "sub", 1) for p in parts]) for p in pair]


def vector_blocks(pair):
    size = lax.axis_size("sub")
    nearest = exchange(pair[: 3 * BS], "sub", 2) if size > 2 else None
    far = []
    for chips in range(2, size // 2, 2):
        far.append(lax.ppermute(pair, "sub", [(i, i ^ (2 * (chips + i % 2))) for i in range(size)]))
    return nearest, far


def near_place(e, core):
    low = e & 1
    same = ((e >> 1) & 1) == core
    return jnp.where(e < 4, e - 1, (e >> 2) * 4 - 1 + jnp.where(same, low, 3 - low))


def after(x, *others):
    return lax.optimization_barrier((x, *others))[0]


def body(
    scalars,
    vectors,
    positions,
    pair_blocks,
    pair_mask,
    wavevectors,
    message_in,
    message_out,
    filter_weight,
    ewald_weight,
    ewald_filter,
    mixing_left,
    mixing_right,
    update_in,
    update_out,
):
    n_region = lax.axis_size("region")
    n_sub = lax.axis_size("sub")
    natoms = BS * n_region * n_sub
    scale = 1.0 / math.sqrt(natoms * KW)
    per_region = pair_blocks.shape[1] // n_region
    slots = -(-min(n_sub - 1, per_region) // 2) * 2
    ids = jnp.stack([lax.axis_index("region"), lax.axis_index("sub")]).astype(jnp.int32)
    place = jnp.pad(positions, ((0, 8 - positions.shape[0]), (0, 0)))
    lean = jnp.concatenate([scalars, place], axis=0)
    vectors = vectors.reshape(3 * BS, -1)
    meta = find_pairs(ids, pair_blocks, n_sub, per_region, slots)
    own_trig = own_trig_of(wavevectors, lean)
    tables = region_trig = spots = None
    for layer in range(LAYERS):
        last = layer == LAYERS - 1
        scalar_parts = from_chips(lean)
        paired = layer == 0
        ahead = (meta, own_trig) if layer == 0 else ()
        if paired:
            beside = exchange(vectors, "sub", 1)
            ahead += (beside,)
        scalar_parts = lax.optimization_barrier((*scalar_parts, *ahead))[: len(scalar_parts)]
        packed = jnp.concatenate(scalar_parts, axis=0)
        blocks = (packed, exchange(packed, "sub", 1))
        own = after(vectors, scalar_parts[1])
        if paired:
            nearest, far = vector_blocks(jnp.concatenate([own, beside], axis=0))
        else:
            near = both_cores(from_chips(own))[1:]
        if layer == 0:
            spots = blocks
            partial, region_trig = structure(layer, n_sub, blocks, ewald_weight, meta, wavevectors)
        else:
            (partial,) = structure(layer, n_sub, blocks, ewald_weight, region_trig=region_trig)
        others = [exchange(partial, "region", mask) for mask in range(1, n_region)]
        weights = (message_in, message_out, filter_weight)
        turn = after(meta, partial, *([] if paired else near[1:2]))
        if layer == 0:
            along, phi, held, held_over, tables = early_terms(turn, layer, n_sub, blocks, spots, weights, masks=pair_mask)
        else:
            along, phi = early_terms(turn, layer, n_sub, blocks, spots, weights, tables=tables, held=held_over)
        others = lax.optimization_barrier((*others, along))[:-1]
        mine = sum(others, partial)
        theirs = exchange(mine, "sub", 1)
        if paired:
            near = [beside]
            for part in ([nearest] if nearest is not None else []) + far:
                part = after(part, along)
                near += [part, exchange(part, "sub", 1)]
        totals = late_terms(meta, layer, paired, phi, near, tables, held, along, filter_weight)
        results = update(
            meta, layer, last, scale, scalars, vectors, totals, mine, theirs, own_trig,
            (ewald_filter, mixing_left, mixing_right, update_in, update_out),
        )
        scalars, vectors = results
        lean = scalars
    return scalars, vectors


def solution(mesh):
    placed = (
        P(("region", "sub"), None),
        P(None, ("region", "sub"), None),
        P(None, ("region", "sub")),
    ) + (P(),) * 12
    return jax.shard_map(
        body,
        mesh=mesh,
        in_specs=placed,
        out_specs=(P(("region", "sub"), None), P(None, ("region", "sub"), None)),
        check_vma=False,
    )
```

```python
import functools
import math

import jax
import jax.numpy as jnp
import numpy as np
from jax import lax
from jax.experimental import pallas as pl
from jax.experimental.pallas import tpu as pltpu
from jax.sharding import PartitionSpec as P

NRBF = 20
BS = 128
KW = 512
LAYERS = 2
BITS = 30
GROUP = 4
CUTOFF = 8.0
SPACING = CUTOFF / (NRBF - 1)
CENTER = 0.5 * CUTOFF
ROOT = math.sqrt(0.5 * math.log2(math.e))
VMEM = 30 * 1024 * 1024
TABLE_SLOTS = 16
WINDOW = 1e10
F32 = jnp.float32
BF16 = jnp.bfloat16


def split(x):
    high = x.astype(BF16)
    return high, (x - high.astype(F32)).astype(BF16)


def wide_left(x):
    high, low = split(x)
    return jnp.concatenate([high, low, high], axis=1)


def wide_right(x):
    high, low = split(x)
    return jnp.concatenate([high, high, low], axis=0)


def stacked(x):
    high, low = split(x)
    return jnp.concatenate([high, high], axis=0), low


def dot(a, b):
    return jnp.dot(a, b, preferred_element_type=F32)


def dot3(a, b):
    return dot(wide_left(a), wide_right(b))


def silu(x):
    return x / (1.0 + jnp.exp(-x))


def turn_fits():
    nodes = 0.5 * np.cos(np.pi * (np.arange(400) + 0.5) / 400)
    cheb = np.polynomial.chebyshev
    fit_cos = cheb.Chebyshev.fit(nodes * nodes, np.cos(2 * np.pi * nodes), 7, domain=[0, 0.25])
    fit_sin = cheb.Chebyshev.fit(nodes * nodes, np.sinc(2 * nodes) * 2 * np.pi, 7, domain=[0, 0.25])
    to_poly = lambda fit: [float(c) for c in fit.convert(kind=np.polynomial.Polynomial).coef]
    return to_poly(fit_cos), to_poly(fit_sin)


COS_FIT, SIN_FIT = turn_fits()


def horner(coefs, x):
    total = jnp.full_like(x, coefs[-1])
    for c in coefs[-2::-1]:
        total = total * x + c
    return total


def cos_sin(turns):
    rest = turns - jnp.round(turns)
    square = rest * rest
    return horner(COS_FIT, square), horner(SIN_FIT, square) * rest


def columns_of(pos):
    return jnp.transpose(pos)


def cost(flops, moved, exps=0):
    return pl.CostEstimate(flops=int(flops), bytes_accessed=int(moved), transcendentals=int(exps))


SMEM_SPEC = pl.BlockSpec(memory_space=pltpu.SMEM)
VMEM_SPEC = pl.BlockSpec(memory_space=pltpu.VMEM)
HBM_SPEC = pl.BlockSpec(memory_space=pltpu.HBM)


def meta_kernel(n_sub, per_region, slots, ids_ref, pairs_ref, meta_ref):
    region, sub = ids_ref[0], ids_ref[1]
    base = region * per_region
    for row in range(6):
        for slot in range(slots):
            meta_ref[row, slot] = lax.rem(sub, 2) if row == 4 else 0

    def visit(p, found):
        first = pairs_ref[0, base + p] - region * n_sub
        second = pairs_ref[1, base + p] - region * n_sub
        hit = (first == sub) | (second == sub)

        @pl.when(hit & (found < slots))
        def _():
            other = jnp.where(first == sub, second, first)
            meta_ref[1, found] = base + p
            meta_ref[2, found] = other ^ sub
            meta_ref[3, found] = (first == sub).astype(jnp.int32)
            meta_ref[5, found] = near_place(other ^ sub, lax.rem(sub, 2))

        return found + hit.astype(jnp.int32)

    meta_ref[0, 0] = lax.fori_loop(0, per_region, visit, jnp.int32(0))


def find_pairs(ids, pair_blocks, n_sub, per_region, slots):
    return pl.pallas_call(
        functools.partial(meta_kernel, n_sub, per_region, slots),
        in_specs=[SMEM_SPEC, SMEM_SPEC],
        out_specs=SMEM_SPEC,
        out_shape=jax.ShapeDtypeStruct((6, slots), jnp.int32),
    )(ids, pair_blocks)


def value_dots(values, sources):
    highs = [v[:, :BS] for v in values]
    both = [b for b, _ in sources]
    low = [l for _, l in sources]
    return dot(jnp.concatenate(values, axis=1), jnp.concatenate(both, axis=0)) + dot(
        jnp.concatenate(highs, axis=1), jnp.concatenate(low, axis=0)
    )


def near_dots(tables, rows, sources):
    return value_dots([tables[i, rows, :] for i in range(len(sources))], sources)


def add_terms(totals, cols, tables, sources, weight):
    total = totals[:, cols]
    for k in range(0, NRBF, GROUP):
        product = near_dots(tables, slice(k * BS, (k + GROUP) * BS), sources)
        total = weigh(total, product, weight, k)
    totals[:, cols] = total


def weigh(total, product, weight, k):
    for g in range(GROUP):
        total = total + product[g * BS : (g + 1) * BS] * weight[k + g : k + g + 1]
    return total


def one_or_two(step, count, act):
    for number in (1, 2):
        here = (2 * step + 1 == count) if number == 1 else (2 * step + 1 < count)
        pl.when(here)(functools.partial(act, number))


def table_copy(table, step, buffer, sems):
    slot = lax.rem(step, 2)
    return pltpu.make_async_copy(table.at[pl.ds(2 * step, 2)], buffer.at[slot], sems.at[slot])


def over_tables(count, table, held, buffer, sems, act):
    steps = (count + 1) // 2
    for back in (3, 4):
        pl.when(steps >= back)(table_copy(table, steps - back, buffer, sems).start)

    def resident(at, carry):
        step = steps - 1 - at
        act(step, held.at[lax.rem(step, 2)], lambda: None)
        return carry

    def one(at, carry):
        step = steps - 1 - at
        act(step, buffer.at[lax.rem(step, 2)], table_copy(table, step, buffer, sems).wait)

        @pl.when(step >= 2)
        def _():
            table_copy(table, step - 2, buffer, sems).start()

        return carry

    lax.fori_loop(0, jnp.minimum(steps, 2), resident, 0)
    lax.fori_loop(2, jnp.maximum(steps, 2), one, 0)


def fill_tables(count, tables, act):
    steps = (count + 1) // 2

    def out(step, table, buffer, sems):
        slot = lax.rem(step, 2)
        return pltpu.make_async_copy(buffer.at[slot], table.at[pl.ds(2 * step, 2)], sems.at[slot])

    def one(step, carry):
        @pl.when(step >= 2)
        def _():
            for t in tables:
                out(step - 2, *t).wait()

        act(step, [buffer.at[lax.rem(step, 2)] for _, buffer, _ in tables])

        @pl.when(step + 2 < steps)
        def _():
            for t in tables:
                out(step, *t).start()

        return carry

    lax.fori_loop(0, steps, one, 0)


def block_views(packed, n_sub):
    chips = n_sub // 2
    height = packed[0].shape[0] // chips
    return [packed[e % 2].at[e // 2 * height : (e // 2 + 1) * height, :] for e in range(n_sub)]


def pair_geometry(meta_ref, listed, near, masks_ref):
    pair = meta_ref[1, listed]
    slot = meta_ref[2, listed]
    is_first = meta_ref[3, listed]
    words = masks_ref[pl.ds(pair, 1), :]
    tiles = -(-words.shape[1] // BS)
    rest = tiles * BS - words.shape[1]
    if rest:
        words = jnp.concatenate([words, jnp.zeros((1, rest), jnp.int32)], axis=1)
    row = lax.broadcasted_iota(jnp.int32, (BS, BS), 0)
    row_tile = (row * 2185) >> 16
    spread = jnp.zeros((BS, BS), jnp.int32)
    for tile in range(tiles):
        spread = jnp.where(
            row_tile == tile,
            jnp.broadcast_to(words[:, tile * BS : (tile + 1) * BS], (BS, BS)),
            spread,
        )
    spot = (row - row_tile * BITS) * BS + lax.broadcasted_iota(jnp.int32, (BS, BS), 1)
    index = (spot * 34953) >> 20
    picked = jnp.take_along_axis(spread, index, axis=1)
    mask = (jnp.right_shift(picked, spot - index * BITS) & 1).astype(F32)
    mask = jnp.where(is_first == 1, mask, jnp.transpose(mask))
    source = jnp.zeros((8, BS), F32)
    for e in range(1, len(near)):
        source = jnp.where(slot == e, near[e][...], source)
    mine = columns_of(near[0][...])
    square = jnp.zeros((BS, BS), F32)
    for d in range(3):
        offset = source[d : d + 1, :] - mine[:, d : d + 1]
        square = square + offset * offset
    distance = jnp.sqrt(square + 1.0)
    inverse = 1.0 / distance
    return jnp.where(mask > 0.5, distance * (ROOT / SPACING), 1.0e4), inverse


def fill_rows(shape, first, at, radial_ref, over_ref):
    scaled, inverse = shape
    kept = []
    for k in range(first, first + GROUP):
        gap = scaled - k * ROOT
        radial = jnp.exp2(-(gap * gap))
        rows = slice(k * BS, (k + 1) * BS)
        for ref, value in ((radial_ref, radial), (over_ref, radial * inverse)):
            high, low = split(value)
            ref[at, rows, 0:BS] = high
            ref[at, rows, BS : 2 * BS] = low
        kept.append(jnp.concatenate([high, low], axis=1))
    return jnp.concatenate(kept, axis=0)


def early_kernel(n_sub, build, layer, meta_ref, *refs):
    blocks = [r.at[:BS, :] for r in block_views(refs[:2], n_sub)]
    places = [r.at[BS:, :] for r in block_views(refs[2:4], n_sub)]
    refs = refs[4:]
    if build:
        in_ref, out_ref, filter_ref, masks_ref, partial_ref, phi_ref, held, held_over, tables_hbm = refs[:9]
        sources, totals, held_sems, over_sems = refs[9:]
    else:
        in_ref, out_ref, filter_ref, tables_hbm, held_over, partial_ref, phi_ref, sources, totals, buffer, sems = refs
    radial_hbm, over_hbm = tables_hbm.at[0], tables_hbm.at[1]
    count = meta_ref[0, 0]
    totals[...] = jnp.zeros_like(totals)
    scalars = jnp.concatenate([blocks[e][...] for e in range(1, n_sub)], axis=0)
    hidden = silu(dot3(scalars, in_ref[layer]))
    phi = dot3(hidden, out_ref[layer])
    for e in range(1, n_sub):
        rows = phi[(e - 1) * BS : e * BS]
        phi_ref[e - 1] = rows[:, : 2 * BS]
        phi_r = rows[:, 2 * BS :]
        place = columns_of(places[e][...])
        parts = [phi_r] + [phi_r * (place[:, d : d + 1] - CENTER) for d in range(3)]
        for at, part in enumerate(parts):
            high, low = split(part)
            cols = slice(at * BS, (at + 1) * BS)
            sources[e - 1, 0:BS, cols] = high
            sources[e - 1, BS : 2 * BS, cols] = high
            sources[e - 1, 2 * BS :, cols] = low

    weight = filter_ref[layer, :, 2 * BS :]
    weight = jnp.concatenate([weight, weight], axis=1)

    def near_sources(step, number, tile):
        cols = slice(tile * 2 * BS, (tile + 1) * 2 * BS)
        slots = [meta_ref[2, 2 * step + i] - 1 for i in range(number)]
        return [(sources[e, : 2 * BS, cols], sources[e, 2 * BS :, cols]) for e in slots]

    if build:

        def terms(step, tables, number):
            shapes = [pair_geometry(meta_ref, 2 * step + i, places, masks_ref) for i in range(number)]
            near = [near_sources(step, number, tile) for tile in range(2)]
            both = [totals[:, tile * 2 * BS : (tile + 1) * 2 * BS] for tile in range(2)]
            for k in range(0, NRBF, GROUP):
                over = [fill_rows(shape, k, i, *tables) for i, shape in enumerate(shapes)]
                for tile in range(2):
                    product = value_dots(over, near[tile])
                    both[tile] = weigh(both[tile], product, weight, k)
            for tile in range(2):
                totals[:, tile * 2 * BS : (tile + 1) * 2 * BS] = both[tile]

        def act(step, tables):
            one_or_two(step, count, functools.partial(terms, step, tables))

        fill_tables(
            count, ((radial_hbm, held, held_sems), (over_hbm, held_over, over_sems)), act
        )
    else:

        def terms(step, table, ready, number):
            ready()
            for tile in range(2):
                cols = slice(tile * 2 * BS, (tile + 1) * 2 * BS)
                add_terms(totals, cols, table, near_sources(step, number, tile), weight)

        def act(step, table, ready):
            one_or_two(step, count, functools.partial(terms, step, table, ready))

        over_tables(count, over_hbm, held_over, buffer, sems, act)

    mine = columns_of(places[0][...])
    for d in range(3):
        partial_ref[d * BS : (d + 1) * BS, :] = (
            totals[:, (1 + d) * BS : (2 + d) * BS] - (mine[:, d : d + 1] - CENTER) * totals[:, :BS]
        )


def table_buffers(number):
    return [pltpu.VMEM((2, 2, NRBF * BS, 2 * BS), BF16), pltpu.SemaphoreType.DMA((2,))] * number


def early_terms(meta, layer, n_sub, blocks, spots, weights, masks=None, tables=None, held=None):
    slots = meta.shape[1]
    build = tables is None
    out_shape = [
        jax.ShapeDtypeStruct((3 * BS, BS), F32),
        jax.ShapeDtypeStruct((n_sub - 1, BS, 2 * BS), F32),
    ]
    two = jax.ShapeDtypeStruct((2, 2, NRBF * BS, 2 * BS), BF16)
    every = jax.ShapeDtypeStruct((2, max(slots, TABLE_SLOTS), NRBF * BS, 2 * BS), BF16)
    return pl.pallas_call(
        functools.partial(early_kernel, n_sub, build, layer),
        in_specs=[SMEM_SPEC] + [VMEM_SPEC] * 7 + ([VMEM_SPEC] if build else [HBM_SPEC, VMEM_SPEC]),
        out_specs=[VMEM_SPEC] * 2 + ([VMEM_SPEC] * 2 + [HBM_SPEC] if build else []),
        scratch_shapes=[
            pltpu.VMEM((n_sub - 1, 3 * BS, 4 * BS), BF16),
            pltpu.VMEM((BS, 4 * BS), F32),
        ]
        + ([pltpu.SemaphoreType.DMA((2,))] * 2 if build else table_buffers(1)),
        out_shape=out_shape + ([two, two, every] if build else []),
        compiler_params=pltpu.CompilerParams(vmem_limit_bytes=VMEM),
        cost_estimate=cost(3 * 4 * NRBF * BS * BS * 4 * BS * 2 * 3, 10e6),
    )(meta, *blocks, *spots, *weights, *((masks,) if build else (tables, held)))


def own_trig_kernel(waves_ref, place_ref, own_ref):
    waves = waves_ref[...] * (1.0 / (2.0 * math.pi))
    mine = columns_of(place_ref[BS:, :])
    turns = jnp.zeros((BS, waves.shape[1]), F32)
    for d in range(3):
        turns = turns + mine[:, d : d + 1] * waves[d : d + 1, :]
    own_ref[...] = jnp.concatenate(split(jnp.concatenate(cos_sin(turns), axis=1)), axis=1)


def own_trig_of(waves, spot):
    return pl.pallas_call(
        own_trig_kernel,
        in_specs=[VMEM_SPEC] * 2,
        out_specs=VMEM_SPEC,
        out_shape=jax.ShapeDtypeStruct((BS, 4 * KW), BF16),
        compiler_params=pltpu.CompilerParams(vmem_limit_bytes=VMEM),
        cost_estimate=cost(WINDOW, 1e6),
    )(waves, spot)


def structure_kernel(n_sub, build, layer, *refs):
    if build:
        meta_ref, waves_ref, refs = refs[0], refs[1], refs[2:]
        places = [r.at[BS:, :] for r in block_views(refs[:2], n_sub)]
    blocks, refs = [r.at[:BS, :] for r in block_views(refs[:2], n_sub)], refs[2:]
    atoms = n_sub * BS
    if build:
        weight_ref, out_ref, trig_ref = refs
        waves = waves_ref[...] * (1.0 / (2.0 * math.pi))
        rows = waves.shape[1] // 2
        waves = jnp.where(meta_ref[4, 0] == 0, waves[:, :rows], waves[:, rows:])
        half = jnp.transpose(jnp.concatenate([waves, jnp.zeros((5, rows), F32)], axis=0))
        for e in range(n_sub):
            place = places[e][...]
            turns = jnp.zeros((rows, BS), F32)
            for d in range(3):
                turns = turns + half[:, d : d + 1] * place[d : d + 1, :]
            for at, value in enumerate(cos_sin(turns)):
                block = slice(at * rows, (at + 1) * rows)
                for part, piece in enumerate(split(value)):
                    trig_ref[block, part * atoms + e * BS : part * atoms + (e + 1) * BS] = piece
    else:
        weight_ref, trig_ref, out_ref = refs
    both, low = stacked(jnp.concatenate([blocks[e][...] for e in range(n_sub)], axis=0))
    total = dot(trig_ref[...], both) + dot(trig_ref[:, :atoms], low)
    out_ref[...] = dot3(total, weight_ref[layer])


def structure(layer, n_sub, blocks, weight, meta=None, waves=None, region_trig=None):
    build = region_trig is None
    out_shape = [jax.ShapeDtypeStruct((KW, BS), F32)]
    if build:
        in_specs = [SMEM_SPEC] + [VMEM_SPEC] * 4
        operands = (meta, waves, *blocks, weight)
        out_shape += [jax.ShapeDtypeStruct((KW, 2 * n_sub * BS), BF16)]
    else:
        in_specs = [VMEM_SPEC] * 4
        operands = (*blocks, weight, region_trig)
    return pl.pallas_call(
        functools.partial(structure_kernel, n_sub, build, layer),
        in_specs=in_specs,
        out_specs=[VMEM_SPEC] * len(out_shape),
        out_shape=out_shape,
        compiler_params=pltpu.CompilerParams(vmem_limit_bytes=VMEM),
        cost_estimate=cost(KW * n_sub * BS * BS * 6, 4e6),
    )(*operands)


def late_kernel(arrays, layer, paired, meta_ref, *refs):
    phi_ref, partial_ref, filter_ref = refs[:3]
    near, refs = refs[3 : 3 + arrays], refs[3 + arrays :]
    near = [r.at[at : at + 3 * BS, :] for r in near for at in range(0, r.shape[0], 3 * BS)]
    tables_hbm, held, totals, buffer, sems = refs
    radial_hbm = tables_hbm.at[0]
    count = meta_ref[0, 0]

    totals[:, :BS] = jnp.zeros((BS, BS), F32)
    for d in range(3):
        totals[:, (1 + d) * BS : (2 + d) * BS] = partial_ref[d * BS : (d + 1) * BS, :]
    w_s, w_v = filter_ref[layer, :, :BS], filter_ref[layer, :, BS : 2 * BS]

    def terms(step, table, ready, number):
        parts = []
        for i in range(number):
            slot = meta_ref[2, 2 * step + i]
            place = meta_ref[5, 2 * step + i] if paired else slot - 1
            vectors = near[0][...]
            for at in range(1, len(near)):
                vectors = jnp.where(place == at, near[at][...], vectors)
            phi = phi_ref[slot - 1]
            phi_s, phi_v = phi[:, :BS], phi[:, BS:]
            parts.append([phi_s] + [phi_v * vectors[d * BS : (d + 1) * BS, :] for d in range(3)])
        sources = [
            [stacked(jnp.concatenate(p[2 * tile : 2 * tile + 2], axis=1)) for p in parts] for tile in range(2)
        ]
        ready()
        for tile, names in enumerate(((w_s, w_v), (w_v, w_v))):
            cols = slice(tile * 2 * BS, (tile + 1) * 2 * BS)
            add_terms(totals, cols, table, sources[tile], jnp.concatenate(names, axis=1))

    def act(step, table, ready):
        one_or_two(step, count, functools.partial(terms, step, table, ready))

    over_tables(count, radial_hbm, held, buffer, sems, act)


def late_terms(meta, layer, paired, phi, near, tables, held, partial, weight):
    arrays = len(near)
    return pl.pallas_call(
        functools.partial(late_kernel, arrays, layer, paired),
        in_specs=[SMEM_SPEC] + [VMEM_SPEC] * (3 + arrays) + [HBM_SPEC, VMEM_SPEC],
        out_specs=VMEM_SPEC,
        scratch_shapes=table_buffers(1),
        out_shape=jax.ShapeDtypeStruct((BS, 4 * BS), F32),
        compiler_params=pltpu.CompilerParams(vmem_limit_bytes=VMEM),
        cost_estimate=cost(3 * 4 * NRBF * BS * BS * 4 * BS * 2 * 3, 10e6),
    )(meta, phi, partial, weight, *near, tables, held)


def update_kernel(scale, layer, last, meta_ref, *refs):
    scalars_ref, vectors_ref, totals, mine_ref, other_ref, own_ref = refs[:6]
    factor_ref, left_ref, right_ref, gate_in_ref, gate_out_ref = refs[6:11]
    outs = refs[11:]
    lower = meta_ref[4, 0] == 0
    mine, other = mine_ref[...], other_ref[...]
    half = mine.shape[0] // 2
    first = jnp.where(lower, mine, other)
    second = jnp.where(lower, other, mine)
    factors = factor_ref[layer] * scale
    both, low = stacked(
        jnp.concatenate(
            [
                first[:half] * factors[:half],
                second[:half] * factors[half:],
                first[half:] * factors[:half],
                second[half:] * factors[half:],
            ],
            axis=0,
        )
    )
    ewald = dot(own_ref[...], both) + dot(own_ref[:, : 2 * KW], low)
    mid_scalars = scalars_ref[...] + totals[:, :BS] + ewald
    mid_vectors = jnp.concatenate(
        [vectors_ref[d * BS : (d + 1) * BS, :] + totals[:, (1 + d) * BS : (2 + d) * BS] for d in range(3)], axis=0
    )
    mixed = dot3(mid_vectors, jnp.concatenate([left_ref[layer], right_ref[layer]], axis=1))
    left, right = mixed[:, :BS], mixed[:, BS:]
    parts = [slice(d * BS, (d + 1) * BS) for d in range(3)]
    norm = jnp.sqrt(sum(right[p] * right[p] for p in parts) + 1.0)
    along = sum(left[p] * right[p] for p in parts)
    hidden = silu(dot3(jnp.concatenate([mid_scalars, norm], axis=1), gate_in_ref[layer]))
    gates = dot3(hidden, gate_out_ref[layer])
    g_v, g_sv, g_s = (gates[:, i * BS : (i + 1) * BS] for i in range(3))
    new_scalars = mid_scalars + g_sv * along + g_s
    new_vectors = [mid_vectors[p] + g_v * left[p] for p in parts]
    if last:
        outs[0][...] = new_scalars
        for d in range(3):
            outs[1][d] = new_vectors[d]
    else:
        outs[0][...] = new_scalars
        for d, p in enumerate(parts):
            outs[1][p, :] = new_vectors[d]


def update(meta, layer, last, scale, scalars, vectors, totals, mine, other, own, weights):
    shapes = [(BS, BS), (3, BS, BS)] if last else [(BS, BS), (3 * BS, BS)]
    return pl.pallas_call(
        functools.partial(update_kernel, scale, layer, last),
        in_specs=[SMEM_SPEC] + [VMEM_SPEC] * 11,
        out_specs=[VMEM_SPEC] * len(shapes),
        out_shape=[jax.ShapeDtypeStruct(shape, F32) for shape in shapes],
        compiler_params=pltpu.CompilerParams(vmem_limit_bytes=VMEM),
        cost_estimate=cost(3e9, 4e6),
    )(meta, scalars, vectors, totals, mine, other, own, *weights)


def exchange(x, axis, mask):
    size = lax.axis_size(axis)
    return lax.ppermute(x, axis, [(i, i ^ mask) for i in range(size)])


def from_chips(x):
    return [x] + [exchange(x, "sub", e) for e in range(2, lax.axis_size("sub"), 2)]


def both_cores(parts):
    return [p for pair in zip(parts, [exchange(p, "sub", 1) for p in parts]) for p in pair]


def vector_blocks(pair):
    size = lax.axis_size("sub")
    nearest = exchange(pair[: 3 * BS], "sub", 2) if size > 2 else None
    far = []
    for chips in range(2, size // 2, 2):
        far.append(lax.ppermute(pair, "sub", [(i, i ^ (2 * (chips + i % 2))) for i in range(size)]))
    return nearest, far


def near_place(e, core):
    low = e & 1
    same = ((e >> 1) & 1) == core
    return jnp.where(e < 4, e - 1, (e >> 2) * 4 - 1 + jnp.where(same, low, 3 - low))


def after(x, *others):
    return lax.optimization_barrier((x, *others))[0]


def body(
    scalars,
    vectors,
    positions,
    pair_blocks,
    pair_mask,
    wavevectors,
    message_in,
    message_out,
    filter_weight,
    ewald_weight,
    ewald_filter,
    mixing_left,
    mixing_right,
    update_in,
    update_out,
):
    n_region = lax.axis_size("region")
    n_sub = lax.axis_size("sub")
    natoms = BS * n_region * n_sub
    scale = 1.0 / math.sqrt(natoms * KW)
    per_region = pair_blocks.shape[1] // n_region
    slots = -(-min(n_sub - 1, per_region) // 2) * 2
    ids = jnp.stack([lax.axis_index("region"), lax.axis_index("sub")]).astype(jnp.int32)
    place = jnp.pad(positions, ((0, 8 - positions.shape[0]), (0, 0)))
    lean = jnp.concatenate([scalars, place], axis=0)
    vectors = vectors.reshape(3 * BS, -1)
    meta = find_pairs(ids, pair_blocks, n_sub, per_region, slots)
    own_trig = own_trig_of(wavevectors, after(lean, meta))
    tables = region_trig = spots = None
    for layer in range(LAYERS):
        last = layer == LAYERS - 1
        scalar_parts = from_chips(lean)
        paired = layer == 0
        ahead = (meta, own_trig) if layer == 0 else ()
        if paired:
            beside = exchange(vectors, "sub", 1)
            ahead += (beside,)
        scalar_parts = lax.optimization_barrier((*scalar_parts, *ahead))[: len(scalar_parts)]
        packed = jnp.concatenate(scalar_parts, axis=0)
        blocks = (packed, exchange(packed, "sub", 1))
        own = after(vectors, scalar_parts[1])
        if paired:
            nearest, far = vector_blocks(jnp.concatenate([own, beside], axis=0))
        else:
            near = both_cores(from_chips(own))[1:]
        if layer == 0:
            spots = blocks
            partial, region_trig = structure(layer, n_sub, blocks, ewald_weight, meta, wavevectors)
        else:
            (partial,) = structure(layer, n_sub, blocks, ewald_weight, region_trig=region_trig)
        others = [exchange(partial, "region", mask) for mask in range(1, n_region)]
        weights = (message_in, message_out, filter_weight)
        turn = after(meta, partial, *([] if paired else near[1:2]))
        if layer == 0:
            along, phi, held, held_over, tables = early_terms(turn, layer, n_sub, blocks, spots, weights, masks=pair_mask)
        else:
            along, phi = early_terms(turn, layer, n_sub, blocks, spots, weights, tables=tables, held=held_over)
        others = lax.optimization_barrier((*others, along))[:-1]
        mine = sum(others, partial)
        theirs = exchange(mine, "sub", 1)
        if paired:
            near = [beside]
            for part in ([nearest] if nearest is not None else []) + far:
                part = after(part, along)
                near += [part, exchange(part, "sub", 1)]
        totals = late_terms(meta, layer, paired, phi, near, tables, held, along, filter_weight)
        results = update(
            meta, layer, last, scale, scalars, vectors, totals, mine, theirs, own_trig,
            (ewald_filter, mixing_left, mixing_right, update_in, update_out),
        )
        scalars, vectors = results
        lean = scalars
    return scalars, vectors


def solution(mesh):
    placed = (
        P(("region", "sub"), None),
        P(None, ("region", "sub"), None),
        P(None, ("region", "sub")),
    ) + (P(),) * 12
    return jax.shard_map(
        body,
        mesh=mesh,
        in_specs=placed,
        out_specs=(P(("region", "sub"), None), P(None, ("region", "sub"), None)),
        check_vma=False,
    )
```
